128 devices in a mesh: gx: 16 (over z_hi, y, core), gy: 8 (over z_lo, x).
Axes of the slice: x: 4, y: 4, z: 4 (z_hi: 2, z_lo: 2; z = z_hi * 2 + z_lo), core: 2. Of those that a mesh axis runs over, the one named last changes fastest.
Arguments:
- pressure: float32 [512, 256, 256], P('gx', 'gy'), may hold values from -6 to 6
- previous: float32 [512, 256, 256], P('gx', 'gy'), may hold values from -6 to 6
- courant: float32 [512, 256, 256], P('gx', 'gy'), may hold values from 0.05 to 0.2
- snapshots: float32 [4, 512, 256, 256], P(None, 'gx', 'gy'), may hold values from -6 to 6
- traces: float32 [128, 128, 4, 128], P(('gx', 'gy')), may hold values from -6 to 6
- cell_offsets: int32 [128, 128, 128], P(('gx', 'gy')), may hold values from 0 to 262143
- live_counts: int32 [128, 128], P(('gx', 'gy')), may hold values from 0 to 128, as said below
Outputs:
- final_pressure: float32 [512, 256, 256], P('gx', 'gy')
- final_previous: float32 [512, 256, 256], P('gx', 'gy')
- image: float32 [512, 256, 256], P('gx', 'gy')
The draws below stay inside these ranges and needn't reach their ends.
Inputs may be any that keep to these rules, and one draw needn't show every extreme that they name: live_counts[s, d] is the number of live slots from device s to subdomain d; in every draw some subdomain receives 128 live slots from every device.
All inputs are finite; a program needn't handle non-finite values.
Results may differ from the reference program's by a relative error of at most 0.00002.
Values sent between devices are 32-bit elements; how exact they have to be, the bound alone decides.
A program may use at most 64 MiB of HBM per device.

```python
import jax
import jax.numpy as jnp

CX = 32
CY = 32
NZ = 256
STEPS = 4
CAP = 128
SUBDOMAINS = 128
NX = 512
NY = 256
N_GY = 8


def draw_live_counts(key, part):
    key = jax.random.fold_in(key, 7)
    key_level, key_raw, key_full = jax.random.split(key, 3)
    level = jax.random.randint(key_level, (SUBDOMAINS,), 1, 5)
    raw = jax.random.randint(key_raw, (SUBDOMAINS, SUBDOMAINS), 0, CAP + 1)
    counts = raw * level[None, :] // 4
    full = jax.random.randint(key_full, (), 0, SUBDOMAINS)
    column = jnp.arange(SUBDOMAINS)[None, :]
    counts = jnp.where(column == full, CAP, counts)
    return counts.astype(jnp.int32)


def set_ends(array, stream_key, low, high):
    longest = array.shape.index(max(array.shape))
    spots = []
    for shift in (0, 1):
        where = [jax.random.randint(jax.random.fold_in(stream_key, axis), (), 0, length) for axis, length in enumerate(array.shape)]
        where[longest] = (where[longest] + shift) % array.shape[longest]
        spots.append(tuple(where))
    return array.at[spots[0]].set(low).at[spots[1]].set(high)


def level_of(rng, extent, shards, least, top_value):
    def one(position, parts):
        draws = jax.random.uniform(jax.random.fold_in(jax.random.fold_in(rng, 6), position), (parts,), jnp.float32, least / len(shards), top_value / len(shards))
        return jnp.repeat(jnp.exp(draws), extent[position] // parts).reshape((-1,) + (1,) * (len(extent) - position - 1))

    loudness = one(*shards[0])
    for cut in shards[1:]:
        loudness = loudness * one(*cut)
    return loudness


def scatter_about(stream_key, extent, spread, bound, shards=(), kind=jnp.bfloat16):
    array = spread * jax.random.normal(stream_key, extent, jnp.float32)
    if shards:
        array = array * level_of(stream_key, extent, shards, -0.22, 0.18)
    return jnp.clip(array, -bound, bound).astype(kind)


def setup_inputs(seed: int = 0) -> dict:
    keys = jax.random.split(jax.random.key(seed), 8)
    return {
        "pressure": scatter_about(keys[0], (NX, NY, NZ), 1.0, 6.0, ((0, 16), (1, 8)), jnp.float32),
        "previous": scatter_about(keys[1], (NX, NY, NZ), 1.0, 6.0, ((0, 16), (1, 8)), jnp.float32),
        "courant": jnp.clip(0.05 + 0.15 * jax.random.uniform(keys[2], (NX, NY, NZ), jnp.float32) ** level_of(keys[2], (NX, NY, NZ), ((0, 16), (1, 8)), -0.2, 0.2), 0.05, 0.2),
        "snapshots": scatter_about(keys[3], (STEPS, NX, NY, NZ), 1.0, 6.0, ((1, 16), (2, 8)), jnp.float32),
        "traces": scatter_about(keys[4], (SUBDOMAINS, SUBDOMAINS, STEPS, CAP), 1.0, 6.0, ((0, 128),), jnp.float32),
        "cell_offsets": set_ends(jax.random.randint(keys[5], (SUBDOMAINS, SUBDOMAINS, CAP), 0, CX * CY * NZ), jax.random.fold_in(keys[5], 1), 0, (CX * CY * NZ) - 1).astype(jnp.int32),
        "live_counts": draw_live_counts(jax.random.fold_in(keys[7], 71), 0),
    }


COEFS = (-205.0 / 72.0, 8.0 / 5.0, -1.0 / 5.0, 8.0 / 315.0, -1.0 / 560.0)


def stencil(padded, width_x, width_y, depth):
    centre = padded[4:4 + width_x, 4:4 + width_y, 4:4 + depth]
    total = (3.0 * COEFS[0]) * centre
    for shift in range(1, 5):
        pairs = padded[4 + shift:4 + shift + width_x, 4:4 + width_y, 4:4 + depth]
        pairs = pairs + padded[4 - shift:4 - shift + width_x, 4:4 + width_y, 4:4 + depth]
        pairs = pairs + padded[4:4 + width_x, 4 + shift:4 + shift + width_y, 4:4 + depth]
        pairs = pairs + padded[4:4 + width_x, 4 - shift:4 - shift + width_y, 4:4 + depth]
        pairs = pairs + padded[4:4 + width_x, 4:4 + width_y, 4 + shift:4 + shift + depth]
        pairs = pairs + padded[4:4 + width_x, 4:4 + width_y, 4 - shift:4 - shift + depth]
        total = total + COEFS[shift] * pairs
    return total


def reference(pressure, previous, courant, snapshots, traces, cell_offsets, live_counts):
    slot = jnp.arange(CAP, dtype=jnp.int32)
    live = slot[None, None, :] < live_counts[:, :, None]
    owner = jnp.arange(SUBDOMAINS, dtype=jnp.int32)
    base_x = (owner // N_GY) * CX
    base_y = (owner % N_GY) * CY
    local_x = cell_offsets // (CY * NZ)
    local_y = (cell_offsets // NZ) % CY
    local_z = cell_offsets % NZ
    glob_x = base_x[None, :, None] + local_x
    glob_y = base_y[None, :, None] + local_y
    flat_cells = ((glob_x * NY + glob_y) * NZ + local_z).astype(jnp.int32).reshape(-1)
    image = jnp.zeros(pressure.shape, jnp.float32)
    for step in range(STEPS):
        padded = jnp.pad(pressure, 4)
        nxt = 2.0 * pressure - previous + courant * stencil(padded, NX, NY, NZ)
        values = jnp.where(live, traces[:, :, step, :], jnp.float32(0.0)).reshape(-1)
        nxt = nxt.reshape(-1).at[flat_cells].add(values).reshape(pressure.shape)
        image = image + snapshots[step] * nxt
        previous = pressure
        pressure = nxt
    return pressure, previous, image
```

```python
import functools

import jax
import jax.numpy as jnp
from jax import lax
from jax.experimental import pallas as pl
from jax.experimental.pallas import tpu as pltpu
from jax.sharding import PartitionSpec as P

STEPS = 4
COEFS = (-205.0 / 72.0, 8.0 / 5.0, -1.0 / 5.0, 8.0 / 315.0, -1.0 / 560.0)
NX, NY = 16, 8
K = 5
ROWS = 8192 + 16
MESH = pl.DeviceIdType.MESH
FIELD = (40, 2, 48, 128)
BLOCK = (32, 2, 32, 128)


def barrier(peers):
    sem = pltpu.get_barrier_semaphore()
    for axis, device in peers:
        pl.semaphore_signal(sem, inc=1, device_id={axis: device}, device_id_type=MESH)
    pl.semaphore_wait(sem, len(peers))


def z_matrix():
    row = lax.broadcasted_iota(jnp.int32, (256, 256), 0)
    col = lax.broadcasted_iota(jnp.int32, (256, 256), 1)
    apart = jnp.abs(row - col)
    matrix = jnp.where(apart == 0, 3.0 * COEFS[0], 0.0)
    for shift in range(1, 5):
        matrix = jnp.where(apart == shift, COEFS[shift], matrix)
    return matrix.astype(jnp.float32)


def z_terms(field, dz, zterm):
    def body(i, _):
        xs = pl.ds(4 + i * 8, 8)
        left = field[xs, 0, pl.ds(8, 32), :].reshape(256, 128)
        right = field[xs, 1, pl.ds(8, 32), :].reshape(256, 128)
        both = jnp.concatenate([left, right], axis=1)
        out = jnp.dot(both, dz[...], precision=lax.Precision.HIGHEST, preferred_element_type=jnp.float32)
        zterm[pl.ds(i * 8, 8), 0] = out[:, :128].reshape(8, 32, 128)
        zterm[pl.ds(i * 8, 8), 1] = out[:, 128:].reshape(8, 32, 128)
        return 0

    lax.fori_loop(0, 4, body, 0)


def laplacian(field, zterm, x, half, tile):
    rows = 8 + tile * 8
    total = zterm[x, half, pl.ds(tile * 8, 8), :]
    for shift in range(1, 5):
        pairs = field[x + 4 + shift, half, pl.ds(rows, 8), :] + field[x + 4 - shift, half, pl.ds(rows, 8), :]
        pairs = pairs + field[x + 4, half, pl.ds(rows + shift, 8), :]
        pairs = pairs + field[x + 4, half, pl.ds(rows - shift, 8), :]
        total = total + COEFS[shift] * pairs
    return total


class Halo:
    def __init__(self, field, ysend, yrecv, sems, index):
        a, b = lax.axis_index("gx"), lax.axis_index("gy")
        self.field, self.ysend, self.yrecv = field, ysend, yrecv
        self.there = (b > 0, b < NY - 1, a > 0, a < NX - 1)
        self.come = (b < NY - 1, b > 0, a < NX - 1, a > 0)
        send, recv = sems

        def copy(d, src, dst, axis, device):
            return pltpu.make_async_remote_copy(
                src_ref=src, dst_ref=dst, send_sem=send.at[index, d], recv_sem=recv.at[index, d],
                device_id={axis: device}, device_id_type=MESH,
            )

        ys = pl.ds(8, 32)
        self.copies = (
            copy(0, ysend.at[0], yrecv.at[0], "gy", b - 1),
            copy(1, ysend.at[1], yrecv.at[1], "gy", b + 1),
            copy(2, field.at[pl.ds(4, 4), :, ys, :], field.at[pl.ds(36, 4), :, ys, :], "gx", a - 1),
            copy(3, field.at[pl.ds(32, 4), :, ys, :], field.at[pl.ds(0, 4), :, ys, :], "gx", a + 1),
        )

    def start(self, d):
        pl.when(self.there[d])(lambda: self.copies[d].start())

    def start_y(self):
        def body(x, _):
            for half in range(2):
                self.ysend[0, x, half] = self.field[x + 4, half, pl.ds(8, 4), :]
                self.ysend[1, x, half] = self.field[x + 4, half, pl.ds(36, 4), :]
            return 0

        lax.fori_loop(0, 32, body, 0)
        self.start(0)
        self.start(1)

    def start_x(self):
        self.start(2)
        self.start(3)

    def wait(self):
        for d in range(4):
            pl.when(self.come[d])(lambda: self.copies[d].wait_recv())
        for d in range(4):
            pl.when(self.there[d])(lambda: self.copies[d].wait_send())

        def body(x, _):
            for half in range(2):
                self.field[x + 4, half, pl.ds(40, 4), :] = self.yrecv[0, x, half]
                self.field[x + 4, half, pl.ds(4, 4), :] = self.yrecv[1, x, half]
            return 0

        lax.fori_loop(0, 32, body, 0)


def clear_edges(field, yrecvs):
    a, b = lax.axis_index("gx"), lax.axis_index("gy")

    @pl.when(a == 0)
    def _():
        field[pl.ds(0, 4)] = jnp.zeros((4,) + FIELD[1:], jnp.float32)

    @pl.when(a == NX - 1)
    def _():
        field[pl.ds(36, 4)] = jnp.zeros((4,) + FIELD[1:], jnp.float32)

    for yrecv in yrecvs:
        @pl.when(b == NY - 1)
        def _():
            yrecv[0] = jnp.zeros((32, 2, 4, 128), jnp.float32)

        @pl.when(b == 0)
        def _():
            yrecv[1] = jnp.zeros((32, 2, 4, 128), jnp.float32)


def deliver_kernel(
    traces, codes, pressure, previous, courant, values_out, codes_out, hom,
    mid_values, mid_codes, field, zterm, dz, ysend, yrecv,
    local_sem, send1, recv1, send2, recv2, hsend, hrecv,
):
    a, b = lax.axis_index("gx"), lax.axis_index("gy")
    sem = pltpu.get_barrier_semaphore()
    peers = [("gy", lax.rem(b + o, NY)) for o in range(1, NY)]
    peers += [("gx", lax.rem(a + o, NX)) for o in range(1, NX)]
    for axis, device in peers:
        pl.semaphore_signal(sem, inc=1, device_id={axis: device}, device_id_type=MESH)

    def load(x, _):
        for half in range(2):
            field[x + 4, half, pl.ds(8, 32), :] = pressure[x, :, half * 128 : half * 128 + 128]
        return 0

    lax.fori_loop(0, 32, load, 0)
    clear_edges(field, [yrecv])
    pl.semaphore_wait(sem, len(peers))

    own1 = [
        pltpu.make_async_copy(traces.at[:, b], mid_values.at[b], local_sem.at[0]),
        pltpu.make_async_copy(codes.at[:, b], mid_codes.at[b], local_sem.at[1]),
    ]
    stage1 = []
    for o in range(1, NY):
        to = lax.rem(b + o, NY)
        for kind, (src, dst) in enumerate(((traces, mid_values), (codes, mid_codes))):
            stage1.append(pltpu.make_async_remote_copy(
                src_ref=src.at[:, to], dst_ref=dst.at[b],
                send_sem=send1.at[o - 1, kind], recv_sem=recv1.at[o - 1, kind],
                device_id={"gy": to}, device_id_type=MESH,
            ))
    for copy in stage1:
        copy.start()
    for copy in own1:
        copy.start()
    halo = Halo(field, ysend, yrecv, (hsend, hrecv), 0)
    halo.start_y()
    halo.start_x()

    dz[...] = z_matrix()
    z_terms(field, dz, zterm)

    for copy in own1:
        copy.wait()
    for copy in stage1:
        copy.wait_recv()

    own2 = [
        pltpu.make_async_copy(mid_values.at[:, a], values_out.at[a], local_sem.at[2]),
        pltpu.make_async_copy(mid_codes.at[:, a], codes_out.at[a], local_sem.at[3]),
    ]
    stage2 = []
    for o in range(1, NX):
        to = lax.rem(a + o, NX)
        for kind, (src, dst) in enumerate(((mid_values, values_out), (mid_codes, codes_out))):
            stage2.append(pltpu.make_async_remote_copy(
                src_ref=src.at[:, to], dst_ref=dst.at[a],
                send_sem=send2.at[o - 1, kind], recv_sem=recv2.at[o - 1, kind],
                device_id={"gx": to}, device_id_type=MESH,
            ))
    for copy in stage2:
        copy.start()
    for copy in own2:
        copy.start()

    halo.wait()

    def step(x, _):
        for half in range(2):
            lanes = pl.ds(half * 128, 128)
            for tile in range(4):
                rows = pl.ds(tile * 8, 8)
                now = field[x + 4, half, pl.ds(8 + tile * 8, 8), :]
                out = 2.0 * now - previous[x, rows, lanes]
                hom[x, half, rows, :] = out + courant[x, rows, lanes] * laplacian(field, zterm, x, half, tile)
        return 0

    lax.fori_loop(0, 32, step, 0)

    for copy in stage1:
        copy.wait_send()
    for copy in own2:
        copy.wait()
    for copy in stage2:
        copy.wait()


def scatter_kernel(codes, values, hom, first, later, *sums):
    zero = jnp.zeros((64, 128), jnp.float32)

    def clear(i, _):
        for total in sums:
            total[pl.ds(pl.multiple_of(i * 64, 64), 64), :] = zero
        return 0

    lax.fori_loop(0, 128, clear, 0)
    for total in sums:
        total[pl.ds(8192, 16), :] = jnp.zeros((16, 128), jnp.float32)
    sub = lax.broadcasted_iota(jnp.int32, (8, 128), 0)
    lane = lax.broadcasted_iota(jnp.int32, (8, 128), 1)
    place = (jnp.where(sub < 4, lane, -1), jnp.where(sub < 4, -1, lane))

    def body(s, _):
        both = jnp.concatenate([values[2 * s], values[2 * s + 1]], axis=0)
        for j in range(128):
            wide = jnp.broadcast_to(both[:, j : j + 1], (8, 128))
            for h in range(2):
                code = codes[2 * s + h, j]
                rows = pl.ds(code >> 8, 8)
                cell = jnp.full((8, 128), code, jnp.int32) & 255
                total = sums[(2 * j + h) % K]
                total[rows, :] = total[rows, :] + jnp.where(place[h] == cell, wide, 0.0)
        return 0

    lax.fori_loop(0, 64, body, 0)

    def finish(i, _):
        rows = pl.ds(pl.multiple_of(i * 64 + 8, 8), 64)
        total = sums[0][rows, :]
        for other in sums[1:]:
            total = total + other[rows, :]
        turned = jnp.swapaxes(total.reshape(8, 8, 128), 0, 1)
        x, ys = i // 4, pl.ds(pl.multiple_of(i % 4 * 8, 8), 8)
        for half in range(2):
            first[x, half, ys, :] = hom[x, half, ys, :] + turned[half * 4]
            for t in range(1, STEPS):
                later[t - 1, x, half, ys, :] = turned[half * 4 + t]
        return 0

    lax.fori_loop(0, 128, finish, 0)


def steps_kernel(
    first, pressure, courant, snapshots, later, out_pressure, out_previous, image,
    field_a, field_b, zterm, dz, ysend, yrecv_a, yrecv_b, hsend, hrecv,
):
    a, b = lax.axis_index("gx"), lax.axis_index("gy")
    sem = pltpu.get_barrier_semaphore()
    near = (("gy", b - 1, b > 0), ("gy", b + 1, b < NY - 1), ("gx", a - 1, a > 0), ("gx", a + 1, a < NX - 1))
    for axis, device, there in near:
        @pl.when(there)
        def _():
            pl.semaphore_signal(sem, inc=1, device_id={axis: device}, device_id_type=MESH)

    def load(x, _):
        for half in range(2):
            lanes = pl.ds(half * 128, 128)
            now = first[x, half]
            field_a[x + 4, half, pl.ds(8, 32), :] = now
            field_b[x + 4, half, pl.ds(8, 32), :] = pressure[x, :, lanes]
            image[x, :, lanes] = snapshots[0, x, :, lanes] * now
        return 0

    lax.fori_loop(0, 32, load, 0)
    clear_edges(field_a, [yrecv_a])
    clear_edges(field_b, [yrecv_b])
    dz[...] = z_matrix()
    pl.semaphore_wait(sem, sum(there.astype(jnp.int32) for _, _, there in near))

    fields, yrecvs = (field_a, field_b), (yrecv_a, yrecv_b)
    halo = Halo(field_a, ysend, yrecv_a, (hsend, hrecv), 0)
    halo.start_y()
    halo.start_x()
    for t in range(1, STEPS):
        now, nxt = fields[(t - 1) % 2], fields[t % 2]
        last = t == STEPS - 1

        def update(x, half, tile):
            lanes, rows, inner = pl.ds(half * 128, 128), pl.ds(tile * 8, 8), pl.ds(8 + tile * 8, 8)
            centre = now[x + 4, half, inner, :]
            out = 2.0 * centre - nxt[x + 4, half, inner, :]
            out = out + courant[x, rows, lanes] * laplacian(now, zterm, x, half, tile)
            out = out + later[t - 1, x, half, rows, :]
            image[x, rows, lanes] = image[x, rows, lanes] + snapshots[t, x, rows, lanes] * out
            if last:
                out_pressure[x, rows, lanes] = out
                out_previous[x, rows, lanes] = centre
            else:
                nxt[x + 4, half, inner, :] = out

        def region(low, high, tiles):
            def body(x, _):
                for half in range(2):
                    for tile in tiles:
                        update(x, half, tile)
                return 0

            lax.fori_loop(low, high, body, 0)

        z_terms(now, dz, zterm)
        region(4, 28, (1, 2))
        halo.wait()
        region(0, 32, (0, 3))
        if not last:
            halo = Halo(nxt, ysend, yrecvs[t % 2], (hsend, hrecv), t)
            halo.start_y()
        region(0, 4, (1, 2))
        region(28, 32, (1, 2))
        if not last:
            halo.start_x()


def local(pressure, previous, courant, snapshots, traces, cell_offsets, live_counts):
    f32 = jnp.float32
    vmem, anywhere = pl.BlockSpec(memory_space=pltpu.VMEM), pl.BlockSpec(memory_space=pl.ANY)
    slot = jnp.arange(128, dtype=jnp.int32)
    live = slot[None, :] < live_counts.reshape(128, 1)
    offsets = cell_offsets.reshape(128, 128)
    margin = 8 - 4 * lax.rem(lax.axis_index("gy"), 2)
    codes = (((offsets >> 7) * 4 + margin) << 8) | (offsets & 127) | jnp.where(live, 0, 128)
    dma, halo_shape = pltpu.SemaphoreType.DMA, (2, 32, 2, 4, 128)
    values, codes, hom = pl.pallas_call(
        deliver_kernel,
        out_shape=(
            jax.ShapeDtypeStruct((NX, NY, 4, 128), f32),
            jax.ShapeDtypeStruct((NX, NY, 1, 128), jnp.int32),
            jax.ShapeDtypeStruct(BLOCK, f32),
        ),
        in_specs=[anywhere, anywhere, vmem, vmem, vmem],
        out_specs=(anywhere, anywhere, vmem),
        scratch_shapes=[
            pltpu.VMEM((NY, NX, 4, 128), f32),
            pltpu.VMEM((NY, NX, 1, 128), jnp.int32),
            pltpu.VMEM(FIELD, f32),
            pltpu.VMEM(BLOCK, f32),
            pltpu.VMEM((256, 256), f32),
            pltpu.VMEM(halo_shape, f32),
            pltpu.VMEM(halo_shape, f32),
            dma((4,)),
            dma((NY - 1, 2)),
            dma((NY - 1, 2)),
            dma((NX - 1, 2)),
            dma((NX - 1, 2)),
            dma((1, 4)),
            dma((1, 4)),
        ],
        compiler_params=pltpu.CompilerParams(
            collective_id=0, has_side_effects=True, vmem_limit_bytes=24 * 2**20
        ),
        name="deliver",
    )(traces.reshape(NX, NY, 4, 128), codes.reshape(NX, NY, 1, 128), pressure, previous, courant)
    first, later = pl.pallas_call(
        scatter_kernel,
        out_shape=(jax.ShapeDtypeStruct(BLOCK, f32), jax.ShapeDtypeStruct((3,) + BLOCK, f32)),
        in_specs=[pl.BlockSpec(memory_space=pltpu.SMEM), vmem, vmem],
        out_specs=(vmem, vmem),
        scratch_shapes=[pltpu.VMEM((ROWS, 128), f32)] * K,
        compiler_params=pltpu.CompilerParams(vmem_limit_bytes=40 * 2**20),
        name="scatter",
    )(codes.reshape(128, 128), values.reshape(128, 4, 128), hom)
    block = jax.ShapeDtypeStruct((32, 32, 256), f32)
    return pl.pallas_call(
        steps_kernel,
        out_shape=(block, block, block),
        in_specs=[vmem] * 5,
        out_specs=(vmem, vmem, vmem),
        scratch_shapes=[
            pltpu.VMEM(FIELD, f32),
            pltpu.VMEM(FIELD, f32),
            pltpu.VMEM(BLOCK, f32),
            pltpu.VMEM((256, 256), f32),
            pltpu.VMEM(halo_shape, f32),
            pltpu.VMEM(halo_shape, f32),
            pltpu.VMEM(halo_shape, f32),
            dma((3, 4)),
            dma((3, 4)),
        ],
        compiler_params=pltpu.CompilerParams(
            collective_id=1, has_side_effects=True, vmem_limit_bytes=40 * 2**20
        ),
        name="steps",
    )(first, pressure, courant, snapshots, later)


def solution(mesh):
    field = P("gx", "gy", None)
    return jax.shard_map(
        local,
        mesh=mesh,
        in_specs=(
            field,
            field,
            field,
            P(None, "gx", "gy", None),
            P(("gx", "gy"), None, None, None),
            P(("gx", "gy"), None, None),
            P(("gx", "gy"), None),
        ),
        out_specs=(field, field, field),
        check_vma=False,
    )
```

```python
import functools

import jax
import jax.numpy as jnp
from jax import lax
from jax.experimental import pallas as pl
from jax.experimental.pallas import tpu as pltpu
from jax.sharding import PartitionSpec as P

STEPS = 4
COEFS = (-205.0 / 72.0, 8.0 / 5.0, -1.0 / 5.0, 8.0 / 315.0, -1.0 / 560.0)
NX, NY = 16, 8
K = 5
ROWS = 8192 + 16
MESH = pl.DeviceIdType.MESH
FIELD = (40, 2, 48, 128)
BLOCK = (32, 2, 32, 128)


def barrier(peers):
    sem = pltpu.get_barrier_semaphore()
    for axis, device in peers:
        pl.semaphore_signal(sem, inc=1, device_id={axis: device}, device_id_type=MESH)
    pl.semaphore_wait(sem, len(peers))


def z_matrix():
    row = lax.broadcasted_iota(jnp.int32, (256, 256), 0)
    col = lax.broadcasted_iota(jnp.int32, (256, 256), 1)
    apart = jnp.abs(row - col)
    matrix = jnp.where(apart == 0, 3.0 * COEFS[0], 0.0)
    for shift in range(1, 5):
        matrix = jnp.where(apart == shift, COEFS[shift], matrix)
    return matrix.astype(jnp.float32)


def z_terms(field, dz, zterm):
    def body(i, _):
        xs = pl.ds(4 + i * 8, 8)
        left = field[xs, 0, pl.ds(8, 32), :].reshape(256, 128)
        right = field[xs, 1, pl.ds(8, 32), :].reshape(256, 128)
        both = jnp.concatenate([left, right], axis=1)
        out = jnp.dot(both, dz[...], precision=lax.Precision.HIGHEST, preferred_element_type=jnp.float32)
        zterm[pl.ds(i * 8, 8), 0] = out[:, :128].reshape(8, 32, 128)
        zterm[pl.ds(i * 8, 8), 1] = out[:, 128:].reshape(8, 32, 128)
        return 0

    lax.fori_loop(0, 4, body, 0)


def laplacian(field, zterm, x, half, tile):
    rows = 8 + tile * 8
    total = zterm[x, half, pl.ds(tile * 8, 8), :]
    for shift in range(1, 5):
        pairs = field[x + 4 + shift, half, pl.ds(rows, 8), :] + field[x + 4 - shift, half, pl.ds(rows, 8), :]
        pairs = pairs + field[x + 4, half, pl.ds(rows + shift, 8), :]
        pairs = pairs + field[x + 4, half, pl.ds(rows - shift, 8), :]
        total = total + COEFS[shift] * pairs
    return total


class Halo:
    def __init__(self, field, ysend, yrecv, sems, index):
        a, b = lax.axis_index("gx"), lax.axis_index("gy")
        self.field, self.ysend, self.yrecv = field, ysend, yrecv
        self.there = (b > 0, b < NY - 1, a > 0, a < NX - 1)
        self.come = (b < NY - 1, b > 0, a < NX - 1, a > 0)
        send, recv = sems

        def copy(d, src, dst, axis, device):
            return pltpu.make_async_remote_copy(
                src_ref=src, dst_ref=dst, send_sem=send.at[index, d], recv_sem=recv.at[index, d],
                device_id={axis: device}, device_id_type=MESH,
            )

        ys = pl.ds(8, 32)
        self.copies = (
            copy(0, ysend.at[0], yrecv.at[0], "gy", b - 1),
            copy(1, ysend.at[1], yrecv.at[1], "gy", b + 1),
            copy(2, field.at[pl.ds(4, 4), :, ys, :], field.at[pl.ds(36, 4), :, ys, :], "gx", a - 1),
            copy(3, field.at[pl.ds(32, 4), :, ys, :], field.at[pl.ds(0, 4), :, ys, :], "gx", a + 1),
        )

    def start(self, d):
        pl.when(self.there[d])(lambda: self.copies[d].start())

    def start_y(self):
        def body(x, _):
            for half in range(2):
                self.ysend[0, x, half] = self.field[x + 4, half, pl.ds(8, 4), :]
                self.ysend[1, x, half] = self.field[x + 4, half, pl.ds(36, 4), :]
            return 0

        lax.fori_loop(0, 32, body, 0)
        self.start(0)
        self.start(1)

    def start_x(self):
        self.start(2)
        self.start(3)

    def wait(self):
        for d in range(4):
            pl.when(self.come[d])(lambda: self.copies[d].wait_recv())
        for d in range(4):
            pl.when(self.there[d])(lambda: self.copies[d].wait_send())

        def body(x, _):
            for half in range(2):
                self.field[x + 4, half, pl.ds(40, 4), :] = self.yrecv[0, x, half]
                self.field[x + 4, half, pl.ds(4, 4), :] = self.yrecv[1, x, half]
            return 0

        lax.fori_loop(0, 32, body, 0)


def clear_edges(field, yrecvs):
    a, b = lax.axis_index("gx"), lax.axis_index("gy")

    @pl.when(a == 0)
    def _():
        field[pl.ds(0, 4)] = jnp.zeros((4,) + FIELD[1:], jnp.float32)

    @pl.when(a == NX - 1)
    def _():
        field[pl.ds(36, 4)] = jnp.zeros((4,) + FIELD[1:], jnp.float32)

    for yrecv in yrecvs:
        @pl.when(b == NY - 1)
        def _():
            yrecv[0] = jnp.zeros((32, 2, 4, 128), jnp.float32)

        @pl.when(b == 0)
        def _():
            yrecv[1] = jnp.zeros((32, 2, 4, 128), jnp.float32)


def deliver_kernel(
    traces, offsets_hbm, live_hbm, pressure_hbm, previous_hbm, courant_hbm,
    values_out, codes_out, hom, pressure, courant,
    offsets, live, codes, previous, mid_values, mid_codes, field, zterm, dz, ysend, yrecv,
    load_sem, local_sem, send1, recv1, send2, recv2, hsend, hrecv,
):
    a, b = lax.axis_index("gx"), lax.axis_index("gy")
    loads = [
        pltpu.make_async_copy(src, dst, load_sem.at[i])
        for i, (src, dst) in enumerate((
            (offsets_hbm, offsets), (live_hbm, live), (pressure_hbm, pressure),
            (previous_hbm, previous), (courant_hbm, courant),
        ))
    ]
    for copy in loads:
        copy.start()
    sem = pltpu.get_barrier_semaphore()
    peers = [("gy", lax.rem(b + o, NY)) for o in range(1, NY)]
    peers += [("gx", lax.rem(a + o, NX)) for o in range(1, NX)]
    for axis, device in peers:
        pl.semaphore_signal(sem, inc=1, device_id={axis: device}, device_id_type=MESH)

    loads[0].wait()
    loads[1].wait()
    lane = lax.broadcasted_iota(jnp.int32, (128, 128), 1)
    counts = jnp.broadcast_to(live[...].astype(jnp.float32), (128, 128)).T.astype(jnp.int32)
    cells = offsets[...]
    margin = 8 - 4 * lax.rem(b, 2)
    code = (((cells >> 7) * 4 + margin) << 8) | (cells & 127) | jnp.where(lane < counts, 0, 128)
    codes[...] = code.reshape(NX, NY, 1, 128)
    clear_edges(field, [yrecv])
    pl.semaphore_wait(sem, len(peers))

    own1 = [
        pltpu.make_async_copy(traces.at[:, b], mid_values.at[b], local_sem.at[0]),
        pltpu.make_async_copy(codes.at[:, b], mid_codes.at[b], local_sem.at[1]),
    ]
    stage1 = []
    for o in range(1, NY):
        to = lax.rem(b + o, NY)
        for kind, (src, dst) in enumerate(((traces, mid_values), (codes, mid_codes))):
            stage1.append(pltpu.make_async_remote_copy(
                src_ref=src.at[:, to], dst_ref=dst.at[b],
                send_sem=send1.at[o - 1, kind], recv_sem=recv1.at[o - 1, kind],
                device_id={"gy": to}, device_id_type=MESH,
            ))
    for copy in stage1:
        copy.start()
    for copy in own1:
        copy.start()
    loads[2].wait()

    def load(x, _):
        for half in range(2):
            field[x + 4, half, pl.ds(8, 32), :] = pressure[x, :, half * 128 : half * 128 + 128]
        return 0

    lax.fori_loop(0, 32, load, 0)
    halo = Halo(field, ysend, yrecv, (hsend, hrecv), 0)
    halo.start_y()
    halo.start_x()

    dz[...] = z_matrix()
    z_terms(field, dz, zterm)

    for copy in own1:
        copy.wait()
    for copy in stage1:
        copy.wait_recv()

    own2 = [
        pltpu.make_async_copy(mid_values.at[:, a], values_out.at[a], local_sem.at[2]),
        pltpu.make_async_copy(mid_codes.at[:, a], codes_out.at[a], local_sem.at[3]),
    ]
    stage2 = []
    for o in range(1, NX):
        to = lax.rem(a + o, NX)
        for kind, (src, dst) in enumerate(((mid_values, values_out), (mid_codes, codes_out))):
            stage2.append(pltpu.make_async_remote_copy(
                src_ref=src.at[:, to], dst_ref=dst.at[a],
                send_sem=send2.at[o - 1, kind], recv_sem=recv2.at[o - 1, kind],
                device_id={"gx": to}, device_id_type=MESH,
            ))
    for copy in stage2:
        copy.start()
    for copy in own2:
        copy.start()

    halo.wait()
    loads[3].wait()
    loads[4].wait()

    def step(x, _):
        for half in range(2):
            lanes = pl.ds(half * 128, 128)
            for tile in range(4):
                rows = pl.ds(tile * 8, 8)
                now = field[x + 4, half, pl.ds(8 + tile * 8, 8), :]
                out = 2.0 * now - previous[x, rows, lanes]
                hom[x, half, rows, :] = out + courant[x, rows, lanes] * laplacian(field, zterm, x, half, tile)
        return 0

    lax.fori_loop(0, 32, step, 0)

    for copy in stage1:
        copy.wait_send()
    for copy in own2:
        copy.wait()
    for copy in stage2:
        copy.wait()


def scatter_kernel(codes, values, hom, first, later, *sums):
    zero = jnp.zeros((64, 128), jnp.float32)

    def clear(i, _):
        for total in sums:
            total[pl.ds(pl.multiple_of(i * 64, 64), 64), :] = zero
        return 0

    lax.fori_loop(0, 128, clear, 0)
    for total in sums:
        total[pl.ds(8192, 16), :] = jnp.zeros((16, 128), jnp.float32)
    sub = lax.broadcasted_iota(jnp.int32, (8, 128), 0)
    lane = lax.broadcasted_iota(jnp.int32, (8, 128), 1)
    place = (jnp.where(sub < 4, lane, -1), jnp.where(sub < 4, -1, lane))

    def body(s, _):
        both = jnp.concatenate([values[2 * s], values[2 * s + 1]], axis=0)
        for j in range(128):
            wide = jnp.broadcast_to(both[:, j : j + 1], (8, 128))
            for h in range(2):
                code = codes[2 * s + h, j]
                rows = pl.ds(code >> 8, 8)
                cell = jnp.full((8, 128), code, jnp.int32) & 255
                total = sums[(2 * j + h) % K]
                total[rows, :] = total[rows, :] + jnp.where(place[h] == cell, wide, 0.0)
        return 0

    lax.fori_loop(0, 64, body, 0)

    def finish(i, _):
        rows = pl.ds(pl.multiple_of(i * 64 + 8, 8), 64)
        total = sums[0][rows, :]
        for other in sums[1:]:
            total = total + other[rows, :]
        turned = jnp.swapaxes(total.reshape(8, 8, 128), 0, 1)
        x, ys = i // 4, pl.ds(pl.multiple_of(i % 4 * 8, 8), 8)
        for half in range(2):
            first[x, half, ys, :] = hom[x, half, ys, :] + turned[half * 4]
            for t in range(1, STEPS):
                later[t - 1, x, half, ys, :] = turned[half * 4 + t]
        return 0

    lax.fori_loop(0, 128, finish, 0)


def steps_kernel(
    first, pressure, courant, snapshots, later, field_a, field_b, zterm, image,
    dz, ysend, yrecv_a, yrecv_b, hsend, hrecv,
):
    a, b = lax.axis_index("gx"), lax.axis_index("gy")
    sem = pltpu.get_barrier_semaphore()
    near = (("gy", b - 1, b > 0), ("gy", b + 1, b < NY - 1), ("gx", a - 1, a > 0), ("gx", a + 1, a < NX - 1))
    for axis, device, there in near:
        @pl.when(there)
        def _():
            pl.semaphore_signal(sem, inc=1, device_id={axis: device}, device_id_type=MESH)

    def load(x, _):
        for half in range(2):
            field_a[x + 4, half, pl.ds(8, 32), :] = first[x, half]
        return 0

    lax.fori_loop(0, 32, load, 0)
    clear_edges(field_a, [yrecv_a])
    clear_edges(field_b, [yrecv_b])
    pl.semaphore_wait(sem, sum(there.astype(jnp.int32) for _, _, there in near))

    fields, yrecvs = (field_a, field_b), (yrecv_a, yrecv_b)
    halo = Halo(field_a, ysend, yrecv_a, (hsend, hrecv), 0)
    halo.start_y()
    halo.start_x()
    dz[...] = z_matrix()

    def load_previous(x, _):
        for half in range(2):
            lanes = pl.ds(half * 128, 128)
            field_b[x + 4, half, pl.ds(8, 32), :] = pressure[x, :, lanes]
            image[x, :, lanes] = snapshots[0, x, :, lanes] * first[x, half]
        return 0

    lax.fori_loop(0, 32, load_previous, 0)
    for t in range(1, STEPS - 1):
        now, nxt = fields[(t - 1) % 2], fields[t % 2]

        def update(x, half, tile):
            lanes, rows, inner = pl.ds(half * 128, 128), pl.ds(tile * 8, 8), pl.ds(8 + tile * 8, 8)
            centre = now[x + 4, half, inner, :]
            out = 2.0 * centre - nxt[x + 4, half, inner, :]
            out = out + courant[x, rows, lanes] * laplacian(now, zterm, x, half, tile)
            out = out + later[t - 1, x, half, rows, :]
            image[x, rows, lanes] = image[x, rows, lanes] + snapshots[t, x, rows, lanes] * out
            nxt[x + 4, half, inner, :] = out

        def region(low, high, tiles):
            def body(x, _):
                for half in range(2):
                    for tile in tiles:
                        update(x, half, tile)
                return 0

            lax.fori_loop(low, high, body, 0)

        z_terms(now, dz, zterm)
        region(4, 28, (1, 2))
        halo.wait()
        region(0, 32, (0, 3))
        halo = Halo(nxt, ysend, yrecvs[t % 2], (hsend, hrecv), t)
        halo.start_y()
        region(0, 4, (1, 2))
        region(28, 32, (1, 2))
        halo.start_x()
    z_terms(fields[STEPS % 2], dz, zterm)
    halo.wait()


def last_kernel(
    now, before, zterm, image_in, later, courant, snapshots, pressure_hbm, previous_hbm, image_hbm,
    pressure, image, out_sem,
):
    stores = [
        pltpu.make_async_copy(
            now.at[pl.ds(4, 32), half, pl.ds(8, 32), :],
            previous_hbm.at[:, :, pl.ds(half * 128, 128)], out_sem.at[half],
        )
        for half in range(2)
    ]
    for copy in stores:
        copy.start()
    for part in range(4):
        def body(x, _):
            for half in range(2):
                for tile in range(4):
                    lanes, rows, inner = pl.ds(half * 128, 128), pl.ds(tile * 8, 8), pl.ds(8 + tile * 8, 8)
                    out = 2.0 * now[x + 4, half, inner, :] - before[x + 4, half, inner, :]
                    out = out + courant[x, rows, lanes] * laplacian(now, zterm, x, half, tile)
                    out = out + later[STEPS - 2, x, half, rows, :]
                    image[x, rows, lanes] = image_in[x, rows, lanes] + snapshots[STEPS - 1, x, rows, lanes] * out
                    pressure[x, rows, lanes] = out
            return 0

        lax.fori_loop(part * 8, part * 8 + 8, body, 0)
        xs = pl.ds(part * 8, 8)
        stores += [
            pltpu.make_async_copy(pressure.at[xs], pressure_hbm.at[xs], out_sem.at[2 + 2 * part]),
            pltpu.make_async_copy(image.at[xs], image_hbm.at[xs], out_sem.at[3 + 2 * part]),
        ]
        stores[-2].start()
        stores[-1].start()
    for copy in stores:
        copy.wait()


def local(pressure, previous, courant, snapshots, traces, cell_offsets, live_counts):
    f32 = jnp.float32
    vmem, anywhere = pl.BlockSpec(memory_space=pltpu.VMEM), pl.BlockSpec(memory_space=pl.ANY)
    hbm = pl.BlockSpec(memory_space=pltpu.HBM)
    dma, halo_shape = pltpu.SemaphoreType.DMA, (2, 32, 2, 4, 128)
    block, wide = jax.ShapeDtypeStruct((32, 32, 256), f32), jax.ShapeDtypeStruct(FIELD, f32)
    values, codes, hom, pressure, courant = pl.pallas_call(
        deliver_kernel,
        out_shape=(
            jax.ShapeDtypeStruct((NX, NY, 4, 128), f32),
            jax.ShapeDtypeStruct((NX, NY, 1, 128), jnp.int32),
            jax.ShapeDtypeStruct(BLOCK, f32),
            block,
            block,
        ),
        in_specs=[hbm] * 6,
        out_specs=(anywhere, anywhere, vmem, vmem, vmem),
        scratch_shapes=[
            pltpu.VMEM((128, 128), jnp.int32),
            pltpu.VMEM((1, 128), jnp.int32),
            pltpu.VMEM((NX, NY, 1, 128), jnp.int32),
            pltpu.VMEM((32, 32, 256), f32),
            pltpu.VMEM((NY, NX, 4, 128), f32),
            pltpu.VMEM((NY, NX, 1, 128), jnp.int32),
            pltpu.VMEM(FIELD, f32),
            pltpu.VMEM(BLOCK, f32),
            pltpu.VMEM((256, 256), f32),
            pltpu.VMEM(halo_shape, f32),
            pltpu.VMEM(halo_shape, f32),
            dma((5,)),
            dma((4,)),
            dma((NY - 1, 2)),
            dma((NY - 1, 2)),
            dma((NX - 1, 2)),
            dma((NX - 1, 2)),
            dma((1, 4)),
            dma((1, 4)),
        ],
        compiler_params=pltpu.CompilerParams(
            collective_id=0, has_side_effects=True, vmem_limit_bytes=51300 * 1024
        ),
        name="deliver",
    )(
        traces.reshape(NX, NY, 4, 128), cell_offsets.reshape(128, 128), live_counts,
        pressure, previous, courant,
    )
    first, later = pl.pallas_call(
        scatter_kernel,
        out_shape=(jax.ShapeDtypeStruct(BLOCK, f32), jax.ShapeDtypeStruct((3,) + BLOCK, f32)),
        in_specs=[pl.BlockSpec(memory_space=pltpu.SMEM), vmem, vmem],
        out_specs=(vmem, vmem),
        scratch_shapes=[pltpu.VMEM((ROWS, 128), f32)] * K,
        compiler_params=pltpu.CompilerParams(vmem_limit_bytes=38000 * 1024),
        name="scatter",
    )(codes.reshape(128, 128), values.reshape(128, 4, 128), hom)
    now, before, zterm, image = pl.pallas_call(
        steps_kernel,
        out_shape=(wide, wide, jax.ShapeDtypeStruct(BLOCK, f32), block),
        in_specs=[vmem] * 5,
        out_specs=(vmem,) * 4,
        scratch_shapes=[
            pltpu.VMEM((256, 256), f32),
            pltpu.VMEM(halo_shape, f32),
            pltpu.VMEM(halo_shape, f32),
            pltpu.VMEM(halo_shape, f32),
            dma((3, 4)),
            dma((3, 4)),
        ],
        compiler_params=pltpu.CompilerParams(
            collective_id=1, has_side_effects=True, vmem_limit_bytes=24000 * 1024
        ),
        name="steps",
    )(first, pressure, courant, snapshots, later)
    return pl.pallas_call(
        last_kernel,
        out_shape=(block, block, block),
        in_specs=[vmem] * 7,
        out_specs=(hbm,) * 3,
        scratch_shapes=[pltpu.VMEM((32, 32, 256), f32)] * 2 + [dma((10,))],
        compiler_params=pltpu.CompilerParams(vmem_limit_bytes=24000 * 1024),
        name="last",
    )(now, before, zterm, image, later, courant, snapshots)


def solution(mesh):
    field = P("gx", "gy", None)
    return jax.shard_map(
        local,
        mesh=mesh,
        in_specs=(
            field,
            field,
            field,
            P(None, "gx", "gy", None),
            P(("gx", "gy"), None, None, None),
            P(("gx", "gy"), None, None),
            P(("gx", "gy"), None),
        ),
        out_specs=(field, field, field),
        check_vma=False,
    )
```

```python
import functools

import jax
import jax.numpy as jnp
from jax import lax
from jax.experimental import pallas as pl
from jax.experimental.pallas import tpu as pltpu
from jax.sharding import PartitionSpec as P

STEPS = 4
COEFS = (-205.0 / 72.0, 8.0 / 5.0, -1.0 / 5.0, 8.0 / 315.0, -1.0 / 560.0)
NX, NY = 16, 8
K = 5
ROWS = 8192 + 16
MESH = pl.DeviceIdType.MESH
FIELD = (40, 2, 48, 128)
BLOCK = (32, 2, 32, 128)


def barrier(peers):
    sem = pltpu.get_barrier_semaphore()
    for axis, device in peers:
        pl.semaphore_signal(sem, inc=1, device_id={axis: device}, device_id_type=MESH)
    pl.semaphore_wait(sem, len(peers))


def z_matrix():
    row = lax.broadcasted_iota(jnp.int32, (256, 256), 0)
    col = lax.broadcasted_iota(jnp.int32, (256, 256), 1)
    apart = jnp.abs(row - col)
    matrix = jnp.where(apart == 0, 3.0 * COEFS[0], 0.0)
    for shift in range(1, 5):
        matrix = jnp.where(apart == shift, COEFS[shift], matrix)
    return matrix.astype(jnp.float32)


def z_terms(field, dz, zterm):
    def body(i, _):
        xs = pl.ds(4 + i * 8, 8)
        left = field[xs, 0, pl.ds(8, 32), :].reshape(256, 128)
        right = field[xs, 1, pl.ds(8, 32), :].reshape(256, 128)
        both = jnp.concatenate([left, right], axis=1)
        out = jnp.dot(both, dz[...], precision=lax.Precision.HIGHEST, preferred_element_type=jnp.float32)
        zterm[pl.ds(i * 8, 8), 0] = out[:, :128].reshape(8, 32, 128)
        zterm[pl.ds(i * 8, 8), 1] = out[:, 128:].reshape(8, 32, 128)
        return 0

    lax.fori_loop(0, 4, body, 0)


def laplacian(field, zterm, x, half, tile):
    rows = 8 + tile * 8
    total = zterm[x, half, pl.ds(tile * 8, 8), :]
    for shift in range(1, 5):
        pairs = field[x + 4 + shift, half, pl.ds(rows, 8), :] + field[x + 4 - shift, half, pl.ds(rows, 8), :]
        pairs = pairs + field[x + 4, half, pl.ds(rows + shift, 8), :]
        pairs = pairs + field[x + 4, half, pl.ds(rows - shift, 8), :]
        total = total + COEFS[shift] * pairs
    return total


class Halo:
    def __init__(self, field, landings, sems, index):
        a, b = lax.axis_index("gx"), lax.axis_index("gy")
        self.there = (b > 0, b < NY - 1, a > 0, a < NX - 1)
        self.come = (b < NY - 1, b > 0, a < NX - 1, a > 0)
        send, recv = sems
        xs, ys = pl.ds(4, 32), pl.ds(8, 32)
        faces = (
            (field.at[xs, :, pl.ds(8, 4), :], "gy", b - 1),
            (field.at[xs, :, pl.ds(36, 4), :], "gy", b + 1),
            (field.at[pl.ds(4, 4), :, ys, :], "gx", a - 1),
            (field.at[pl.ds(32, 4), :, ys, :], "gx", a + 1),
        )
        self.copies = [
            pltpu.make_async_remote_copy(
                src_ref=face, dst_ref=landing, send_sem=send.at[index, d], recv_sem=recv.at[index, d],
                device_id={axis: device}, device_id_type=MESH,
            )
            for d, ((face, axis, device), landing) in enumerate(zip(faces, landings))
        ]

    def start(self):
        for d in range(4):
            pl.when(self.there[d])(lambda: self.copies[d].start())

    def wait(self):
        for d in range(4):
            pl.when(self.come[d])(lambda: self.copies[d].wait_recv())
        for d in range(4):
            pl.when(self.there[d])(lambda: self.copies[d].wait_send())


def field_landings(field):
    xs, ys = pl.ds(4, 32), pl.ds(8, 32)
    return (
        field.at[xs, :, pl.ds(40, 4), :], field.at[xs, :, pl.ds(4, 4), :],
        field.at[pl.ds(36, 4), :, ys, :], field.at[pl.ds(0, 4), :, ys, :],
    )


def side_landings(xside, yside):
    return yside.at[1, :, :, pl.ds(8, 4), :], yside.at[0, :, :, pl.ds(4, 4), :], xside.at[1], xside.at[0]


def clear_field_edges(field):
    a, b = lax.axis_index("gx"), lax.axis_index("gy")
    for edge, low in ((a == 0, 0), (a == NX - 1, 36)):
        @pl.when(edge)
        def _():
            field[pl.ds(low, 4)] = jnp.zeros((4,) + FIELD[1:], jnp.float32)

    for edge, low in ((b == 0, 0), (b == NY - 1, 40)):
        @pl.when(edge)
        def _():
            field[:, :, pl.ds(low, 8), :] = jnp.zeros((40, 2, 8, 128), jnp.float32)


def clear_halo(field):
    for low in (0, 36):
        field[pl.ds(low, 4)] = jnp.zeros((4,) + FIELD[1:], jnp.float32)
    for low in (0, 40):
        field[pl.ds(4, 32), :, pl.ds(low, 8), :] = jnp.zeros((32, 2, 8, 128), jnp.float32)


def clear_sides(xside, yside):
    a, b = lax.axis_index("gx"), lax.axis_index("gy")
    rows = jnp.zeros((32, 2, 8, 128), jnp.float32)
    yside[0, :, :, pl.ds(8, 8), :] = rows
    yside[1, :, :, pl.ds(0, 8), :] = rows
    for edge, side, low in ((b == 0, 0, 0), (b == NY - 1, 1, 8)):
        @pl.when(edge)
        def _():
            yside[side, :, :, pl.ds(low, 8), :] = rows

    for edge, side in ((a == 0, 0), (a == NX - 1, 1)):
        @pl.when(edge)
        def _():
            xside[side] = jnp.zeros((4, 2, 32, 128), jnp.float32)


def y_face_terms(yside, x, half, tile):
    total = None
    for shift in range(1, 5):
        low = 8 - shift if tile == 0 else shift
        term = COEFS[shift] * yside[0 if tile == 0 else 1, x, half, pl.ds(low, 8), :]
        total = term if total is None else total + term
    return total


def x_face_terms(xside, side, layer, half, tile):
    total = None
    for shift in range(layer + 1, 5):
        there = 4 + layer - shift if side == 0 else shift - layer - 1
        term = COEFS[shift] * xside[side, there, half, pl.ds(tile * 8, 8), :]
        total = term if total is None else total + term
    return total


def deliver_kernel(
    traces, offsets_hbm, live_hbm, pressure_hbm, previous_hbm, courant_hbm,
    values_out, codes_out, hom, pressure, courant,
    offsets, live, codes, previous, mid_values0, mid_values1, mid_codes0, mid_codes1, field, zterm, dz,
    load_sem, local_sem, send1, recv1, send2, recv2, send3, recv3, send4, recv4, hsend, hrecv,
):
    a, b = lax.axis_index("gx"), lax.axis_index("gy")
    loads = [
        pltpu.make_async_copy(src, dst, load_sem.at[i])
        for i, (src, dst) in enumerate((
            (offsets_hbm, offsets), (live_hbm, live), (pressure_hbm, pressure),
            (previous_hbm, previous), (courant_hbm, courant),
        ))
    ]
    for copy in loads:
        copy.start()
    sem = pltpu.get_barrier_semaphore()
    peers = [("gy", lax.rem(b + o, NY)) for o in range(1, NY)]
    peers += [("gx", lax.rem(a + o, NX)) for o in range(1, NX)]
    for axis, device in peers:
        pl.semaphore_signal(sem, inc=1, device_id={axis: device}, device_id_type=MESH)

    loads[0].wait()
    loads[1].wait()
    lane = lax.broadcasted_iota(jnp.int32, (128, 128), 1)
    counts = jnp.broadcast_to(live[...].astype(jnp.float32), (128, 128)).T.astype(jnp.int32)
    cells = offsets[...]
    margin = 8 - 4 * lax.rem(b, 2)
    code = (((cells >> 7) * 4 + margin) << 8) | (cells & 127) | jnp.where(lane < counts, 0, 128)
    codes[...] = code.reshape(8, 2, NY, 1, 128)
    clear_field_edges(field)
    pl.semaphore_wait(sem, len(peers))

    core, pair = lax.rem(a, 2), a // 2
    both = ((traces, mid_values0, mid_values1, values_out), (codes, mid_codes0, mid_codes1, codes_out))

    def remote(src, dst, send, recv, device):
        return pltpu.make_async_remote_copy(
            src_ref=src, dst_ref=dst, send_sem=send, recv_sem=recv, device_id=device, device_id_type=MESH
        )

    gy_first, gx_first, gx_second, gy_second = [], [], [], []
    own_first, own_second, own_gx_first, own_gx_second = [], [], [], []
    for kind, (given, mid0, mid1, out) in enumerate(both):
        own_first.append(pltpu.make_async_copy(given.at[:, 0, b], mid0.at[b], local_sem.at[0, kind]))
        own_gx_first.append(pltpu.make_async_copy(given.at[pair, 1], mid1.at[a], local_sem.at[1, kind]))
        own_gx_second.append(pltpu.make_async_copy(mid0.at[:, pair], out.at[a], local_sem.at[2, kind]))
        own_second.append(pltpu.make_async_copy(mid1.at[:, b], out.at[:, b], local_sem.at[3, kind]))
    for o in range(1, NY):
        to = lax.rem(b + o, NY)
        for kind, (given, mid0, mid1, out) in enumerate(both):
            gy_first.append(remote(
                given.at[:, 0, to], mid0.at[b], send1.at[o - 1, kind], recv1.at[o - 1, kind], {"gy": to}
            ))
            gy_second.append(remote(
                mid1.at[:, to], out.at[:, b], send4.at[o - 1, kind], recv4.at[o - 1, kind], {"gy": to}
            ))
    for o in range(8):
        to = lax.rem(pair + o, 8)
        for kind, (given, mid0, mid1, out) in enumerate(both):
            gx_first.append(remote(
                given.at[to, 1], mid1.at[a], send2.at[o, kind], recv2.at[o, core, kind], {"gx": 2 * to + 1}
            ))
            gx_second.append(remote(
                mid0.at[:, to], out.at[a], send3.at[o, kind], recv3.at[o, core, kind], {"gx": 2 * to}
            ))

    def gx_arrived(recv, landing):
        for o in range(8):
            for sender in range(2):
                for kind in range(2):
                    def wait():
                        remote(
                            landing[kind], landing[kind], send2.at[o, kind], recv.at[o, sender, kind], {"gx": a}
                        ).wait_recv()

                    if o > 0:
                        wait()
                    else:
                        pl.when(core != sender)(wait)

    for n in range(16):
        if n < 14:
            gy_first[n].start()
        if n >= 2:
            gx_first[n].start()
    for copy in own_first:
        copy.start()

    @pl.when(core == 0)
    def _():
        gx_first[0].start()
        gx_first[1].start()

    @pl.when(core == 1)
    def _():
        own_gx_first[0].start()
        own_gx_first[1].start()

    loads[2].wait()

    def load(x, _):
        for half in range(2):
            field[x + 4, half, pl.ds(8, 32), :] = pressure[x, :, half * 128 : half * 128 + 128]
        return 0

    lax.fori_loop(0, 32, load, 0)
    halo = Halo(field, field_landings(field), (hsend, hrecv), 0)
    halo.start()

    dz[...] = z_matrix()
    z_terms(field, dz, zterm)

    for copy in own_first:
        copy.wait()
    for copy in gy_first:
        copy.wait_recv()
    for copy in gx_second[2:]:
        copy.start()

    @pl.when(core == 0)
    def _():
        own_gx_second[0].start()
        own_gx_second[1].start()

    @pl.when(core == 1)
    def _():
        gx_second[0].start()
        gx_second[1].start()
        own_gx_first[0].wait()
        own_gx_first[1].wait()
        gx_arrived(recv2, (mid_values1.at[0], mid_codes1.at[0]))
        for copy in gy_second:
            copy.start()
        for copy in own_second:
            copy.start()

    halo.wait()
    loads[3].wait()
    loads[4].wait()

    def step(x, _):
        for half in range(2):
            lanes = pl.ds(half * 128, 128)
            for tile in range(4):
                rows = pl.ds(tile * 8, 8)
                now = field[x + 4, half, pl.ds(8 + tile * 8, 8), :]
                out = 2.0 * now - previous[x, rows, lanes]
                hom[x, half, rows, :] = out + courant[x, rows, lanes] * laplacian(field, zterm, x, half, tile)
        return 0

    lax.fori_loop(0, 32, step, 0)

    for copy in gy_first:
        copy.wait_send()
    for copy in gx_first[2:]:
        copy.wait_send()
    for copy in gx_second[2:]:
        copy.wait_send()

    @pl.when(core == 0)
    def _():
        gx_first[0].wait_send()
        gx_first[1].wait_send()
        own_gx_second[0].wait()
        own_gx_second[1].wait()
        gx_arrived(recv3, (values_out.at[0], codes_out.at[0]))

    @pl.when(core == 1)
    def _():
        gx_second[0].wait_send()
        gx_second[1].wait_send()
        for copy in own_second:
            copy.wait()
        for copy in gy_second:
            copy.wait()


def scatter_kernel(codes, values, hom, first, later, *sums):
    zero = jnp.zeros((64, 128), jnp.float32)

    def clear(i, _):
        for total in sums:
            total[pl.ds(pl.multiple_of(i * 64, 64), 64), :] = zero
        return 0

    lax.fori_loop(0, 128, clear, 0)
    for total in sums:
        total[pl.ds(8192, 16), :] = jnp.zeros((16, 128), jnp.float32)
    sub = lax.broadcasted_iota(jnp.int32, (8, 128), 0)
    lane = lax.broadcasted_iota(jnp.int32, (8, 128), 1)
    place = (jnp.where(sub < 4, lane, -1), jnp.where(sub < 4, -1, lane))

    def body(s, _):
        both = jnp.concatenate([values[2 * s], values[2 * s + 1]], axis=0)
        for j in range(128):
            wide = jnp.broadcast_to(both[:, j : j + 1], (8, 128))
            for h in range(2):
                code = codes[2 * s + h, j]
                rows = pl.ds(code >> 8, 8)
                cell = jnp.full((8, 128), code, jnp.int32) & 255
                total = sums[(2 * j + h) % K]
                total[rows, :] = total[rows, :] + jnp.where(place[h] == cell, wide, 0.0)
        return 0

    lax.fori_loop(0, 64, body, 0)

    def finish(i, _):
        rows = pl.ds(pl.multiple_of(i * 64 + 8, 8), 64)
        total = sums[0][rows, :]
        for other in sums[1:]:
            total = total + other[rows, :]
        turned = jnp.swapaxes(total.reshape(8, 8, 128), 0, 1)
        x, ys = i // 4, pl.ds(pl.multiple_of(i % 4 * 8, 8), 8)
        for half in range(2):
            first[x, half, ys, :] = hom[x, half, ys, :] + turned[half * 4]
            for t in range(1, STEPS):
                later[t - 1, x, half, ys, :] = turned[half * 4 + t]
        return 0

    lax.fori_loop(0, 128, finish, 0)


def steps_kernel(
    first, pressure, courant, snapshots, later, field_a, out, image, xside_a, yside_a,
    field_b, zterm, dz, xside_b, yside_b, hsend, hrecv,
):
    a, b = lax.axis_index("gx"), lax.axis_index("gy")
    sem = pltpu.get_barrier_semaphore()
    near = (("gy", b - 1, b > 0), ("gy", b + 1, b < NY - 1), ("gx", a - 1, a > 0), ("gx", a + 1, a < NX - 1))
    for axis, device, there in near:
        @pl.when(there)
        def _():
            pl.semaphore_signal(sem, inc=1, device_id={axis: device}, device_id_type=MESH)

    def load(x, _):
        for half in range(2):
            field_a[x + 4, half, pl.ds(8, 32), :] = first[x, half]
        return 0

    lax.fori_loop(0, 32, load, 0)
    pl.semaphore_wait(sem, sum(there.astype(jnp.int32) for _, _, there in near))

    fields, sides = (field_a, field_b), ((xside_a, yside_a), (xside_b, yside_b))
    halo = Halo(field_a, side_landings(xside_a, yside_a), (hsend, hrecv), 0)
    halo.start()
    for field in fields:
        clear_halo(field)
    for side in sides:
        clear_sides(*side)
    dz[...] = z_matrix()

    for t in range(1, STEPS):
        now, nxt = fields[(t - 1) % 2], fields[t % 2]
        xside, yside = sides[(t - 1) % 2]
        last = t == STEPS - 1
        z_terms(now, dz, zterm)

        def update(x, _):
            for half in range(2):
                lanes = pl.ds(half * 128, 128)
                for tile in range(4):
                    rows, inner = pl.ds(tile * 8, 8), pl.ds(8 + tile * 8, 8)
                    centre = now[x + 4, half, inner, :]
                    before = pressure[x, rows, lanes] if t == 1 else nxt[x + 4, half, inner, :]
                    new = 2.0 * centre - before
                    new = new + courant[x, rows, lanes] * laplacian(now, zterm, x, half, tile)
                    new = new + later[t - 1, x, half, rows, :]
                    seen = snapshots[0, x, rows, lanes] * centre if t == 1 else image[x, rows, lanes]
                    image[x, rows, lanes] = seen + snapshots[t, x, rows, lanes] * new
                    if last:
                        out[x, rows, lanes] = new
                    else:
                        nxt[x + 4, half, inner, :] = new
            return 0

        lax.fori_loop(0, 32, update, 0)
        halo.wait()
        if last:
            break

        def add(x, half, tile, terms):
            lanes, rows, inner = pl.ds(half * 128, 128), pl.ds(tile * 8, 8), pl.ds(8 + tile * 8, 8)
            more = courant[x, rows, lanes] * terms
            nxt[x + 4, half, inner, :] = nxt[x + 4, half, inner, :] + more
            image[x, rows, lanes] = image[x, rows, lanes] + snapshots[t, x, rows, lanes] * more

        def y_faces(x, _):
            for half in range(2):
                for tile in (0, 3):
                    add(x, half, tile, y_face_terms(yside, x, half, tile))
            return 0

        def x_faces(tile, _):
            for half in range(2):
                for side in range(2):
                    for layer in range(4):
                        x = layer if side == 0 else 31 - layer
                        add(x, half, tile, x_face_terms(xside, side, layer, half, tile))
            return 0

        lax.fori_loop(0, 32, y_faces, 0)
        lax.fori_loop(0, 4, x_faces, 0)
        halo = Halo(nxt, side_landings(*sides[t % 2]), (hsend, hrecv), t)
        halo.start()


def last_kernel(
    now, out, image_in, xside, yside, courant, snapshots, pressure_hbm, previous_hbm, image_hbm,
    pressure, image, out_sem,
):
    stores = [
        pltpu.make_async_copy(
            now.at[pl.ds(4, 32), half, pl.ds(8, 32), :],
            previous_hbm.at[:, :, pl.ds(half * 128, 128)], out_sem.at[half],
        )
        for half in range(2)
    ]
    for copy in stores:
        copy.start()

    def one(x, side, layer):
        for half in range(2):
            for tile in range(4):
                lanes, rows = pl.ds(half * 128, 128), pl.ds(tile * 8, 8)
                new, seen = out[x, rows, lanes], image_in[x, rows, lanes]
                terms = y_face_terms(yside, x, half, tile) if tile in (0, 3) else None
                if layer is not None:
                    more = x_face_terms(xside, side, layer, half, tile)
                    terms = more if terms is None else terms + more
                if terms is not None:
                    more = courant[x, rows, lanes] * terms
                    new = new + more
                    seen = seen + snapshots[STEPS - 1, x, rows, lanes] * more
                pressure[x, rows, lanes] = new
                image[x, rows, lanes] = seen

    def body(x, _):
        one(x, None, None)
        return 0

    for part in range(4):
        if part == 0:
            for layer in range(4):
                one(layer, 0, layer)
        lax.fori_loop(max(4, part * 8), min(28, part * 8 + 8), body, 0)
        if part == 3:
            for layer in range(4):
                one(31 - layer, 1, layer)
        xs = pl.ds(part * 8, 8)
        stores += [
            pltpu.make_async_copy(pressure.at[xs], pressure_hbm.at[xs], out_sem.at[2 + 2 * part]),
            pltpu.make_async_copy(image.at[xs], image_hbm.at[xs], out_sem.at[3 + 2 * part]),
        ]
        stores[-2].start()
        stores[-1].start()
    for copy in stores:
        copy.wait()


def local(pressure, previous, courant, snapshots, traces, cell_offsets, live_counts):
    f32 = jnp.float32
    vmem, anywhere = pl.BlockSpec(memory_space=pltpu.VMEM), pl.BlockSpec(memory_space=pl.ANY)
    hbm = pl.BlockSpec(memory_space=pltpu.HBM)
    dma, xside, yside = pltpu.SemaphoreType.DMA, (2, 4, 2, 32, 128), (2, 32, 2, 16, 128)
    block, wide = jax.ShapeDtypeStruct((32, 32, 256), f32), jax.ShapeDtypeStruct(FIELD, f32)
    values, codes, hom, pressure, courant = pl.pallas_call(
        deliver_kernel,
        out_shape=(
            jax.ShapeDtypeStruct((NX, NY, 4, 128), f32),
            jax.ShapeDtypeStruct((NX, NY, 1, 128), jnp.int32),
            jax.ShapeDtypeStruct(BLOCK, f32),
            block,
            block,
        ),
        in_specs=[hbm] * 6,
        out_specs=(anywhere, anywhere, vmem, vmem, vmem),
        scratch_shapes=[
            pltpu.VMEM((128, 128), jnp.int32),
            pltpu.VMEM((1, 128), jnp.int32),
            pltpu.VMEM((8, 2, NY, 1, 128), jnp.int32),
            pltpu.VMEM((32, 32, 256), f32),
            pltpu.VMEM((NY, 8, 4, 128), f32),
            pltpu.VMEM((NX, NY, 4, 128), f32),
            pltpu.VMEM((NY, 8, 1, 128), jnp.int32),
            pltpu.VMEM((NX, NY, 1, 128), jnp.int32),
            pltpu.VMEM(FIELD, f32),
            pltpu.VMEM(BLOCK, f32),
            pltpu.VMEM((256, 256), f32),
            dma((5,)),
            dma((4, 2)),
            dma((NY - 1, 2)),
            dma((NY - 1, 2)),
            dma((8, 2)),
            dma((8, 2, 2)),
            dma((8, 2)),
            dma((8, 2, 2)),
            dma((NY - 1, 2)),
            dma((NY - 1, 2)),
            dma((1, 4)),
            dma((1, 4)),
        ],
        compiler_params=pltpu.CompilerParams(
            collective_id=0, has_side_effects=True, vmem_limit_bytes=51300 * 1024
        ),
        name="deliver",
    )(
        traces.reshape(8, 2, NY, 4, 128), cell_offsets.reshape(128, 128), live_counts,
        pressure, previous, courant,
    )
    first, later = pl.pallas_call(
        scatter_kernel,
        out_shape=(jax.ShapeDtypeStruct(BLOCK, f32), jax.ShapeDtypeStruct((3,) + BLOCK, f32)),
        in_specs=[pl.BlockSpec(memory_space=pltpu.SMEM), vmem, vmem],
        out_specs=(vmem, vmem),
        scratch_shapes=[pltpu.VMEM((ROWS, 128), f32)] * K,
        compiler_params=pltpu.CompilerParams(vmem_limit_bytes=38000 * 1024),
        name="scatter",
    )(codes.reshape(128, 128), values.reshape(128, 4, 128), hom)
    now, out, image, xfaces, yfaces = pl.pallas_call(
        steps_kernel,
        out_shape=(wide, block, block, jax.ShapeDtypeStruct(xside, f32), jax.ShapeDtypeStruct(yside, f32)),
        in_specs=[vmem] * 5,
        out_specs=(vmem,) * 5,
        scratch_shapes=[
            pltpu.VMEM(FIELD, f32),
            pltpu.VMEM(BLOCK, f32),
            pltpu.VMEM((256, 256), f32),
            pltpu.VMEM(xside, f32),
            pltpu.VMEM(yside, f32),
            dma((3, 4)),
            dma((3, 4)),
        ],
        compiler_params=pltpu.CompilerParams(
            collective_id=1, has_side_effects=True, vmem_limit_bytes=24000 * 1024
        ),
        name="steps",
    )(first, pressure, courant, snapshots, later)
    return pl.pallas_call(
        last_kernel,
        out_shape=(block, block, block),
        in_specs=[vmem] * 7,
        out_specs=(hbm,) * 3,
        scratch_shapes=[pltpu.VMEM((32, 32, 256), f32)] * 2 + [dma((10,))],
        compiler_params=pltpu.CompilerParams(vmem_limit_bytes=24000 * 1024),
        name="last",
    )(now, out, image, xfaces, yfaces, courant, snapshots)


def solution(mesh):
    field = P("gx", "gy", None)
    return jax.shard_map(
        local,
        mesh=mesh,
        in_specs=(
            field,
            field,
            field,
            P(None, "gx", "gy", None),
            P(("gx", "gy"), None, None, None),
            P(("gx", "gy"), None, None),
            P(("gx", "gy"), None),
        ),
        out_specs=(field, field, field),
        check_vma=False,
    )
```

```python
import functools

import jax
import jax.numpy as jnp
from jax import lax
from jax.experimental import pallas as pl
from jax.experimental.pallas import tpu as pltpu
from jax.sharding import PartitionSpec as P

STEPS = 4
COEFS = (-205.0 / 72.0, 8.0 / 5.0, -1.0 / 5.0, 8.0 / 315.0, -1.0 / 560.0)
NX, NY = 16, 8
K = 6
ROWS = 8192 + 16
MESH = pl.DeviceIdType.MESH
FIELD = (40, 2, 48, 128)
BLOCK = (32, 2, 32, 128)


def barrier(peers):
    sem = pltpu.get_barrier_semaphore()
    for axis, device in peers:
        pl.semaphore_signal(sem, inc=1, device_id={axis: device}, device_id_type=MESH)
    pl.semaphore_wait(sem, len(peers))


def z_matrix():
    row = lax.broadcasted_iota(jnp.int32, (256, 256), 0)
    col = lax.broadcasted_iota(jnp.int32, (256, 256), 1)
    apart = jnp.abs(row - col)
    matrix = jnp.where(apart == 0, 3.0 * COEFS[0], 0.0)
    for shift in range(1, 5):
        matrix = jnp.where(apart == shift, COEFS[shift], matrix)
    return matrix.astype(jnp.float32)


def z_terms(field, dz, zterm):
    def body(i, _):
        xs = pl.ds(4 + i * 8, 8)
        left = field[xs, 0, pl.ds(8, 32), :].reshape(256, 128)
        right = field[xs, 1, pl.ds(8, 32), :].reshape(256, 128)
        both = jnp.concatenate([left, right], axis=1)
        out = jnp.dot(both, dz[...], precision=lax.Precision.HIGHEST, preferred_element_type=jnp.float32)
        zterm[pl.ds(i * 8, 8), 0] = out[:, :128].reshape(8, 32, 128)
        zterm[pl.ds(i * 8, 8), 1] = out[:, 128:].reshape(8, 32, 128)
        return 0

    lax.fori_loop(0, 4, body, 0)


def laplacian(field, zterm, x, half, tile):
    rows = 8 + tile * 8
    total = zterm[x, half, pl.ds(tile * 8, 8), :]
    for shift in range(1, 5):
        pairs = field[x + 4 + shift, half, pl.ds(rows, 8), :] + field[x + 4 - shift, half, pl.ds(rows, 8), :]
        pairs = pairs + field[x + 4, half, pl.ds(rows + shift, 8), :]
        pairs = pairs + field[x + 4, half, pl.ds(rows - shift, 8), :]
        total = total + COEFS[shift] * pairs
    return total


class Halo:
    def __init__(self, field, landings, sems, index):
        a, b = lax.axis_index("gx"), lax.axis_index("gy")
        self.there = (b > 0, b < NY - 1, a > 0, a < NX - 1)
        self.come = (b < NY - 1, b > 0, a < NX - 1, a > 0)
        send, recv = sems
        xs, ys = pl.ds(4, 32), pl.ds(8, 32)
        faces = (
            (field.at[xs, :, pl.ds(8, 4), :], "gy", b - 1),
            (field.at[xs, :, pl.ds(36, 4), :], "gy", b + 1),
            (field.at[pl.ds(4, 4), :, ys, :], "gx", a - 1),
            (field.at[pl.ds(32, 4), :, ys, :], "gx", a + 1),
        )
        self.copies = [
            pltpu.make_async_remote_copy(
                src_ref=face, dst_ref=landing, send_sem=send.at[index, d], recv_sem=recv.at[index, d],
                device_id={axis: device}, device_id_type=MESH,
            )
            for d, ((face, axis, device), landing) in enumerate(zip(faces, landings))
        ]

    def start(self):
        for d in range(4):
            pl.when(self.there[d])(lambda: self.copies[d].start())

    def wait(self):
        for d in range(4):
            pl.when(self.come[d])(lambda: self.copies[d].wait_recv())
        for d in range(4):
            pl.when(self.there[d])(lambda: self.copies[d].wait_send())


def field_landings(field):
    xs, ys = pl.ds(4, 32), pl.ds(8, 32)
    return (
        field.at[xs, :, pl.ds(40, 4), :], field.at[xs, :, pl.ds(4, 4), :],
        field.at[pl.ds(36, 4), :, ys, :], field.at[pl.ds(0, 4), :, ys, :],
    )


def side_landings(xside, yside):
    return yside.at[1, :, :, pl.ds(8, 4), :], yside.at[0, :, :, pl.ds(4, 4), :], xside.at[1], xside.at[0]


def clear_field_edges(field):
    a, b = lax.axis_index("gx"), lax.axis_index("gy")
    for edge, low in ((a == 0, 0), (a == NX - 1, 36)):
        @pl.when(edge)
        def _():
            field[pl.ds(low, 4)] = jnp.zeros((4,) + FIELD[1:], jnp.float32)

    for edge, low in ((b == 0, 0), (b == NY - 1, 40)):
        @pl.when(edge)
        def _():
            field[:, :, pl.ds(low, 8), :] = jnp.zeros((40, 2, 8, 128), jnp.float32)


def clear_halo(field):
    for low in (0, 36):
        field[pl.ds(low, 4)] = jnp.zeros((4,) + FIELD[1:], jnp.float32)
    for low in (0, 40):
        field[pl.ds(4, 32), :, pl.ds(low, 8), :] = jnp.zeros((32, 2, 8, 128), jnp.float32)


def clear_sides(xside, yside):
    a, b = lax.axis_index("gx"), lax.axis_index("gy")
    rows = jnp.zeros((32, 2, 8, 128), jnp.float32)
    yside[0, :, :, pl.ds(8, 8), :] = rows
    yside[1, :, :, pl.ds(0, 8), :] = rows
    for edge, side, low in ((b == 0, 0, 0), (b == NY - 1, 1, 8)):
        @pl.when(edge)
        def _():
            yside[side, :, :, pl.ds(low, 8), :] = rows

    for edge, side in ((a == 0, 0), (a == NX - 1, 1)):
        @pl.when(edge)
        def _():
            xside[side] = jnp.zeros((4, 2, 32, 128), jnp.float32)


def y_face_terms(yside, x, half, tile):
    total = None
    for shift in range(1, 5):
        low = 8 - shift if tile == 0 else shift
        term = COEFS[shift] * yside[0 if tile == 0 else 1, x, half, pl.ds(low, 8), :]
        total = term if total is None else total + term
    return total


def x_face_terms(xside, side, layer, half, tile):
    total = None
    for shift in range(layer + 1, 5):
        there = 4 + layer - shift if side == 0 else shift - layer - 1
        term = COEFS[shift] * xside[side, there, half, pl.ds(tile * 8, 8), :]
        total = term if total is None else total + term
    return total


def deliver_kernel(
    traces, offsets_hbm, live_hbm, pressure_hbm, previous_hbm, courant_hbm,
    values_out, codes_out, hom, pressure, courant,
    offsets, live, codes, previous, mid_values0, mid_values1, mid_codes0, mid_codes1, field, zterm, dz,
    load_sem, local_sem, send1, recv1, send2, recv2, send3, recv3, send4, recv4, hsend, hrecv,
):
    a, b = lax.axis_index("gx"), lax.axis_index("gy")
    loads = [
        pltpu.make_async_copy(src, dst, load_sem.at[i])
        for i, (src, dst) in enumerate((
            (offsets_hbm, offsets), (live_hbm, live), (pressure_hbm, pressure),
            (previous_hbm, previous), (courant_hbm, courant),
        ))
    ]
    for copy in loads:
        copy.start()
    sem = pltpu.get_barrier_semaphore()
    peers = [("gy", lax.rem(b + o, NY)) for o in range(1, NY)]
    peers += [("gx", lax.rem(a + o, NX)) for o in range(1, NX)]
    for axis, device in peers:
        pl.semaphore_signal(sem, inc=1, device_id={axis: device}, device_id_type=MESH)

    loads[0].wait()
    loads[1].wait()
    lane = lax.broadcasted_iota(jnp.int32, (128, 128), 1)
    counts = jnp.broadcast_to(live[...].astype(jnp.float32), (128, 128)).T.astype(jnp.int32)
    cells = offsets[...]
    margin = 8 - 4 * lax.rem(b, 2)
    code = (((cells >> 7) * 4 + margin) << 8) | jnp.where(lane < counts, cells & 127, 255)
    codes[...] = code.reshape(8, 2, NY, 1, 128)
    clear_field_edges(field)
    pl.semaphore_wait(sem, len(peers))

    core, pair = lax.rem(a, 2), a // 2
    both = ((traces, mid_values0, mid_values1, values_out), (codes, mid_codes0, mid_codes1, codes_out))

    def remote(src, dst, send, recv, device):
        return pltpu.make_async_remote_copy(
            src_ref=src, dst_ref=dst, send_sem=send, recv_sem=recv, device_id=device, device_id_type=MESH
        )

    gy_first, gx_first, gx_second, gy_second = [], [], [], []
    own_first, own_second, own_gx_first, own_gx_second = [], [], [], []
    for kind, (given, mid0, mid1, out) in enumerate(both):
        own_first.append(pltpu.make_async_copy(given.at[:, 0, b], mid0.at[b], local_sem.at[0, kind]))
        own_gx_first.append(pltpu.make_async_copy(given.at[pair, 1], mid1.at[a], local_sem.at[1, kind]))
        own_gx_second.append(pltpu.make_async_copy(mid0.at[:, pair], out.at[a], local_sem.at[2, kind]))
        own_second.append(pltpu.make_async_copy(mid1.at[:, b], out.at[:, b], local_sem.at[3, kind]))
    for o in range(1, NY):
        to = lax.rem(b + o, NY)
        for kind, (given, mid0, mid1, out) in enumerate(both):
            gy_first.append(remote(
                given.at[:, 0, to], mid0.at[b], send1.at[o - 1, kind], recv1.at[o - 1, kind], {"gy": to}
            ))
            gy_second.append(remote(
                mid1.at[:, to], out.at[:, b], send4.at[o - 1, kind], recv4.at[o - 1, kind], {"gy": to}
            ))
    for o in range(8):
        to = lax.rem(pair + o, 8)
        for kind, (given, mid0, mid1, out) in enumerate(both):
            gx_first.append(remote(
                given.at[to, 1], mid1.at[a], send2.at[o, kind], recv2.at[o, core, kind], {"gx": 2 * to + 1}
            ))
            gx_second.append(remote(
                mid0.at[:, to], out.at[a], send3.at[o, kind], recv3.at[o, core, kind], {"gx": 2 * to}
            ))

    def gx_arrived(recv, landing):
        for o in range(8):
            for sender in range(2):
                for kind in range(2):
                    def wait():
                        remote(
                            landing[kind], landing[kind], send2.at[o, kind], recv.at[o, sender, kind], {"gx": a}
                        ).wait_recv()

                    if o > 0:
                        wait()
                    else:
                        pl.when(core != sender)(wait)

    for n in range(16):
        if n < 14:
            gy_first[n].start()
        if n >= 2:
            gx_first[n].start()
    for copy in own_first:
        copy.start()

    @pl.when(core == 0)
    def _():
        gx_first[0].start()
        gx_first[1].start()

    @pl.when(core == 1)
    def _():
        own_gx_first[0].start()
        own_gx_first[1].start()

    loads[2].wait()

    def load(x, _):
        for half in range(2):
            field[x + 4, half, pl.ds(8, 32), :] = pressure[x, :, half * 128 : half * 128 + 128]
        return 0

    lax.fori_loop(0, 32, load, 0)
    halo = Halo(field, field_landings(field), (hsend, hrecv), 0)
    halo.start()

    dz[...] = z_matrix()
    z_terms(field, dz, zterm)

    for copy in own_first:
        copy.wait()
    for copy in gy_first:
        copy.wait_recv()
    for copy in gx_second[2:]:
        copy.start()

    @pl.when(core == 0)
    def _():
        own_gx_second[0].start()
        own_gx_second[1].start()

    @pl.when(core == 1)
    def _():
        gx_second[0].start()
        gx_second[1].start()
        own_gx_first[0].wait()
        own_gx_first[1].wait()
        gx_arrived(recv2, (mid_values1.at[0], mid_codes1.at[0]))
        for copy in gy_second:
            copy.start()
        for copy in own_second:
            copy.start()

    halo.wait()
    loads[3].wait()
    loads[4].wait()

    def step(x, _):
        for half in range(2):
            lanes = pl.ds(half * 128, 128)
            for tile in range(4):
                rows = pl.ds(tile * 8, 8)
                now = field[x + 4, half, pl.ds(8 + tile * 8, 8), :]
                out = 2.0 * now - previous[x, rows, lanes]
                hom[x, half, rows, :] = out + courant[x, rows, lanes] * laplacian(field, zterm, x, half, tile)
        return 0

    lax.fori_loop(0, 32, step, 0)

    for copy in gy_first:
        copy.wait_send()
    for copy in gx_first[2:]:
        copy.wait_send()
    for copy in gx_second[2:]:
        copy.wait_send()

    @pl.when(core == 0)
    def _():
        gx_first[0].wait_send()
        gx_first[1].wait_send()
        own_gx_second[0].wait()
        own_gx_second[1].wait()
        gx_arrived(recv3, (values_out.at[0], codes_out.at[0]))

    @pl.when(core == 1)
    def _():
        gx_second[0].wait_send()
        gx_second[1].wait_send()
        for copy in own_second:
            copy.wait()
        for copy in gy_second:
            copy.wait()


def clear_sums(sums):
    zero = jnp.zeros((64, 128), jnp.float32)

    def clear(i, _):
        for total in sums:
            total[pl.ds(pl.multiple_of(i * 64, 64), 64), :] = zero
        return 0

    lax.fori_loop(0, 128, clear, 0)
    for total in sums:
        total[pl.ds(8192, 16), :] = jnp.zeros((16, 128), jnp.float32)


def scatter_kernel(codes, values, *rest):
    sums = rest[:K]
    rows_all, lanes_all, rows0, rows1, lanes0, lanes1, sems = rest[K:]
    rows_all[...] = codes[...] >> 8
    word = codes[pl.ds(0, 32, stride=4), :] & 255
    for q in range(1, 4):
        word = word | ((codes[pl.ds(q, 32, stride=4), :] & 255) << (8 * q))
    lanes_all[...] = word
    blocks = ((rows0, lanes0), (rows1, lanes1))

    def fetch(group, n):
        rows, lanes = blocks[n]
        return (
            pltpu.make_async_copy(rows_all.at[pl.ds(4 * group, 4)], rows, sems.at[n, 0]),
            pltpu.make_async_copy(lanes_all.at[pl.ds(group, 1)], lanes, sems.at[n, 1]),
        )

    for n in range(2):
        for copy in fetch(n, n):
            copy.start()
    clear_sums(sums)
    sub = lax.broadcasted_iota(jnp.int32, (8, 128), 0)
    lane = lax.broadcasted_iota(jnp.int32, (8, 128), 1)
    place = (jnp.where(sub < 4, lane, 128), jnp.where(sub < 4, 128, lane))
    place = [place[q % 2] << (8 * q) for q in range(4)]
    bits = (255, 255 << 8, 255 << 16, -(1 << 24))

    def body(i, _):
        for n in range(2):
            group = 2 * i + n
            for copy in fetch(group, n):
                copy.wait()
            rows, lanes = blocks[n]
            pairs = [
                jnp.concatenate([values[4 * group + 2 * p], values[4 * group + 2 * p + 1]], axis=0) for p in range(2)
            ]
            for j in range(128):
                wide = [jnp.broadcast_to(pair[:, j : j + 1], (8, 128)) for pair in pairs]
                cells = jnp.full((8, 128), lanes[0, j], jnp.int32)
                for q in range(4):
                    window = pl.ds(rows[q, j], 8)
                    total = sums[(4 * j + q) % K]
                    more = jnp.where((cells & bits[q]) == place[q], wide[q // 2], 0.0)
                    total[window, :] = total[window, :] + more

            @pl.when(i < 15)
            def _():
                for copy in fetch(group + 2, n):
                    copy.start()
        return 0

    lax.fori_loop(0, 16, body, 0)


def steps_kernel(
    *refs,
):
    sums, refs = refs[:K], refs[K:]
    (hom, pressure, courant, field_a, field_b, first, out, xside_a, yside_a, later,
     zterm, dz, xside_b, yside_b, hsend, hrecv) = refs
    a, b = lax.axis_index("gx"), lax.axis_index("gy")
    sem = pltpu.get_barrier_semaphore()
    near = (("gy", b - 1, b > 0), ("gy", b + 1, b < NY - 1), ("gx", a - 1, a > 0), ("gx", a + 1, a < NX - 1))
    for axis, device, there in near:
        @pl.when(there)
        def _():
            pl.semaphore_signal(sem, inc=1, device_id={axis: device}, device_id_type=MESH)

    def finish(i, _):
        rows = pl.ds(pl.multiple_of(i * 64 + 8, 8), 64)
        total = sums[0][rows, :]
        for other in sums[1:]:
            total = total + other[rows, :]
        turned = jnp.swapaxes(total.reshape(8, 8, 128), 0, 1)
        x, y = i // 4, i % 4 * 8
        for half in range(2):
            ys = pl.ds(pl.multiple_of(y, 8), 8)
            new = hom[x, half, ys, :] + turned[half * 4]
            first[x, half, ys, :] = new
            field_a[x + 4, half, pl.ds(pl.multiple_of(y + 8, 8), 8), :] = new
            for t in range(1, STEPS):
                later[t - 1, x, half, ys, :] = turned[half * 4 + t]
        return 0

    lax.fori_loop(0, 128, finish, 0)
    pl.semaphore_wait(sem, sum(there.astype(jnp.int32) for _, _, there in near))

    fields, sides = (field_a, field_b), ((xside_a, yside_a), (xside_b, yside_b))
    halo = Halo(field_a, side_landings(xside_a, yside_a), (hsend, hrecv), 0)
    halo.start()
    for field in fields:
        clear_halo(field)
    for side in sides:
        clear_sides(*side)
    dz[...] = z_matrix()

    for t in range(1, STEPS):
        now, nxt = fields[(t - 1) % 2], fields[t % 2]
        xside, yside = sides[(t - 1) % 2]
        last = t == STEPS - 1
        z_terms(now, dz, zterm)

        def update(x, _):
            for half in range(2):
                lanes = pl.ds(half * 128, 128)
                for tile in range(4):
                    rows, inner = pl.ds(tile * 8, 8), pl.ds(8 + tile * 8, 8)
                    centre = now[x + 4, half, inner, :]
                    before = pressure[x, rows, lanes] if t == 1 else nxt[x + 4, half, inner, :]
                    new = 2.0 * centre - before
                    new = new + courant[x, rows, lanes] * laplacian(now, zterm, x, half, tile)
                    new = new + later[t - 1, x, half, rows, :]
                    if last:
                        out[x, rows, lanes] = new
                    else:
                        nxt[x + 4, half, inner, :] = new
            return 0

        lax.fori_loop(0, 32, update, 0)
        halo.wait()
        if last:
            break

        def add(x, half, tile, terms):
            lanes, rows, inner = pl.ds(half * 128, 128), pl.ds(tile * 8, 8), pl.ds(8 + tile * 8, 8)
            more = courant[x, rows, lanes] * terms
            nxt[x + 4, half, inner, :] = nxt[x + 4, half, inner, :] + more

        def y_faces(x, _):
            for half in range(2):
                for tile in (0, 3):
                    add(x, half, tile, y_face_terms(yside, x, half, tile))
            return 0

        def x_faces(tile, _):
            for half in range(2):
                for side in range(2):
                    for layer in range(4):
                        x = layer if side == 0 else 31 - layer
                        add(x, half, tile, x_face_terms(xside, side, layer, half, tile))
            return 0

        lax.fori_loop(0, 32, y_faces, 0)
        lax.fori_loop(0, 4, x_faces, 0)
        halo = Halo(nxt, side_landings(*sides[t % 2]), (hsend, hrecv), t)
        halo.start()


def last_kernel(
    now, before, first, out, xside, yside, courant, snapshots, pressure_hbm, previous_hbm, image_hbm,
    pressure, image, out_sem,
):
    stores = [
        pltpu.make_async_copy(
            now.at[pl.ds(4, 32), half, pl.ds(8, 32), :],
            previous_hbm.at[:, :, pl.ds(half * 128, 128)], out_sem.at[half],
        )
        for half in range(2)
    ]
    for copy in stores:
        copy.start()

    def one(x, side, layer):
        for half in range(2):
            for tile in range(4):
                lanes, rows = pl.ds(half * 128, 128), pl.ds(tile * 8, 8)
                inner = pl.ds(8 + tile * 8, 8)
                new = out[x, rows, lanes]
                terms = y_face_terms(yside, x, half, tile) if tile in (0, 3) else None
                if layer is not None:
                    more = x_face_terms(xside, side, layer, half, tile)
                    terms = more if terms is None else terms + more
                if terms is not None:
                    new = new + courant[x, rows, lanes] * terms
                pressure[x, rows, lanes] = new
                seen = snapshots[0, x, rows, lanes] * first[x, half, rows, :]
                seen = seen + snapshots[1, x, rows, lanes] * before[x + 4, half, inner, :]
                seen = seen + snapshots[2, x, rows, lanes] * now[x + 4, half, inner, :]
                image[x, rows, lanes] = seen + snapshots[3, x, rows, lanes] * new

    def body(x, _):
        one(x, None, None)
        return 0

    for part in range(4):
        if part == 0:
            for layer in range(4):
                one(layer, 0, layer)
        lax.fori_loop(max(4, part * 8), min(28, part * 8 + 8), body, 0)
        if part == 3:
            for layer in range(4):
                one(31 - layer, 1, layer)
        xs = pl.ds(part * 8, 8)
        stores += [
            pltpu.make_async_copy(pressure.at[xs], pressure_hbm.at[xs], out_sem.at[2 + 2 * part]),
            pltpu.make_async_copy(image.at[xs], image_hbm.at[xs], out_sem.at[3 + 2 * part]),
        ]
        stores[-2].start()
        stores[-1].start()
    for copy in stores:
        copy.wait()


def local(pressure, previous, courant, snapshots, traces, cell_offsets, live_counts):
    f32 = jnp.float32
    vmem, anywhere = pl.BlockSpec(memory_space=pltpu.VMEM), pl.BlockSpec(memory_space=pl.ANY)
    hbm = pl.BlockSpec(memory_space=pltpu.HBM)
    dma, xside, yside = pltpu.SemaphoreType.DMA, (2, 4, 2, 32, 128), (2, 32, 2, 16, 128)
    block, wide = jax.ShapeDtypeStruct((32, 32, 256), f32), jax.ShapeDtypeStruct(FIELD, f32)
    values, codes, hom, pressure, courant = pl.pallas_call(
        deliver_kernel,
        out_shape=(
            jax.ShapeDtypeStruct((NX, NY, 4, 128), f32),
            jax.ShapeDtypeStruct((NX, NY, 1, 128), jnp.int32),
            jax.ShapeDtypeStruct(BLOCK, f32),
            block,
            block,
        ),
        in_specs=[hbm] * 6,
        out_specs=(anywhere, anywhere, vmem, vmem, vmem),
        scratch_shapes=[
            pltpu.VMEM((128, 128), jnp.int32),
            pltpu.VMEM((1, 128), jnp.int32),
            pltpu.VMEM((8, 2, NY, 1, 128), jnp.int32),
            pltpu.VMEM((32, 32, 256), f32),
            pltpu.VMEM((NY, 8, 4, 128), f32),
            pltpu.VMEM((NX, NY, 4, 128), f32),
            pltpu.VMEM((NY, 8, 1, 128), jnp.int32),
            pltpu.VMEM((NX, NY, 1, 128), jnp.int32),
            pltpu.VMEM(FIELD, f32),
            pltpu.VMEM(BLOCK, f32),
            pltpu.VMEM((256, 256), f32),
            dma((5,)),
            dma((4, 2)),
            dma((NY - 1, 2)),
            dma((NY - 1, 2)),
            dma((8, 2)),
            dma((8, 2, 2)),
            dma((8, 2)),
            dma((8, 2, 2)),
            dma((NY - 1, 2)),
            dma((NY - 1, 2)),
            dma((1, 4)),
            dma((1, 4)),
        ],
        compiler_params=pltpu.CompilerParams(
            collective_id=0, has_side_effects=True, vmem_limit_bytes=51300 * 1024
        ),
        name="deliver",
    )(
        traces.reshape(8, 2, NY, 4, 128), cell_offsets.reshape(128, 128), live_counts,
        pressure, previous, courant,
    )
    sums = pl.pallas_call(
        scatter_kernel,
        out_shape=(jax.ShapeDtypeStruct((ROWS, 128), f32),) * K,
        in_specs=[vmem, vmem],
        out_specs=(vmem,) * K,
        scratch_shapes=[
            pltpu.VMEM((128, 128), jnp.int32),
            pltpu.VMEM((32, 128), jnp.int32),
            pltpu.SMEM((4, 128), jnp.int32),
            pltpu.SMEM((4, 128), jnp.int32),
            pltpu.SMEM((1, 128), jnp.int32),
            pltpu.SMEM((1, 128), jnp.int32),
            dma((2, 2)),
        ],
        compiler_params=pltpu.CompilerParams(vmem_limit_bytes=8000 * 1024),
        name="scatter",
    )(codes.reshape(128, 128), values.reshape(128, 4, 128))
    now, before, first, out, xfaces, yfaces = pl.pallas_call(
        steps_kernel,
        out_shape=(
            wide,
            wide,
            jax.ShapeDtypeStruct(BLOCK, f32),
            block,
            jax.ShapeDtypeStruct(xside, f32),
            jax.ShapeDtypeStruct(yside, f32),
        ),
        in_specs=[vmem] * (K + 3),
        out_specs=(vmem,) * 6,
        scratch_shapes=[
            pltpu.VMEM((3,) + BLOCK, f32),
            pltpu.VMEM(BLOCK, f32),
            pltpu.VMEM((256, 256), f32),
            pltpu.VMEM(xside, f32),
            pltpu.VMEM(yside, f32),
            dma((3, 4)),
            dma((3, 4)),
        ],
        compiler_params=pltpu.CompilerParams(
            collective_id=1, has_side_effects=True, vmem_limit_bytes=10000 * 1024
        ),
        name="steps",
    )(*sums, hom, pressure, courant)
    return pl.pallas_call(
        last_kernel,
        out_shape=(block, block, block),
        in_specs=[vmem] * 8,
        out_specs=(hbm,) * 3,
        scratch_shapes=[pltpu.VMEM((32, 32, 256), f32)] * 2 + [dma((10,))],
        compiler_params=pltpu.CompilerParams(vmem_limit_bytes=6000 * 1024),
        name="last",
    )(now, before, first, out, xfaces, yfaces, courant, snapshots)


def solution(mesh):
    field = P("gx", "gy", None)
    return jax.shard_map(
        local,
        mesh=mesh,
        in_specs=(
            field,
            field,
            field,
            P(None, "gx", "gy", None),
            P(("gx", "gy"), None, None, None),
            P(("gx", "gy"), None, None),
            P(("gx", "gy"), None),
        ),
        out_specs=(field, field, field),
        check_vma=False,
    )
```

```python
import functools

import jax
import jax.numpy as jnp
from jax import lax
from jax.experimental import pallas as pl
from jax.experimental.pallas import tpu as pltpu
from jax.sharding import PartitionSpec as P

STEPS = 4
COEFS = (-205.0 / 72.0, 8.0 / 5.0, -1.0 / 5.0, 8.0 / 315.0, -1.0 / 560.0)
NX, NY = 16, 8
K = 6
ROWS = 8192 + 16
MESH = pl.DeviceIdType.MESH
FIELD = (40, 2, 48, 128)
BLOCK = (32, 2, 32, 128)


def barrier(peers):
    sem = pltpu.get_barrier_semaphore()
    for axis, device in peers:
        pl.semaphore_signal(sem, inc=1, device_id={axis: device}, device_id_type=MESH)
    pl.semaphore_wait(sem, len(peers))


def z_matrix():
    row = lax.broadcasted_iota(jnp.int32, (256, 256), 0)
    col = lax.broadcasted_iota(jnp.int32, (256, 256), 1)
    apart = jnp.abs(row - col)
    matrix = jnp.where(apart == 0, 3.0 * COEFS[0], 0.0)
    for shift in range(1, 5):
        matrix = jnp.where(apart == shift, COEFS[shift], matrix)
    return matrix.astype(jnp.float32)


def z_terms(field, dz, zterm):
    def body(i, _):
        xs = pl.ds(4 + i * 8, 8)
        left = field[xs, 0, pl.ds(8, 32), :].reshape(256, 128)
        right = field[xs, 1, pl.ds(8, 32), :].reshape(256, 128)
        both = jnp.concatenate([left, right], axis=1)
        out = jnp.dot(both, dz[...], precision=lax.Precision.HIGHEST, preferred_element_type=jnp.float32)
        zterm[pl.ds(i * 8, 8), 0] = out[:, :128].reshape(8, 32, 128)
        zterm[pl.ds(i * 8, 8), 1] = out[:, 128:].reshape(8, 32, 128)
        return 0

    lax.fori_loop(0, 4, body, 0)


def laplacian(field, zterm, x, half, tile):
    rows = 8 + tile * 8
    total = zterm[x, half, pl.ds(tile * 8, 8), :]
    for shift in range(1, 5):
        pairs = field[x + 4 + shift, half, pl.ds(rows, 8), :] + field[x + 4 - shift, half, pl.ds(rows, 8), :]
        pairs = pairs + field[x + 4, half, pl.ds(rows + shift, 8), :]
        pairs = pairs + field[x + 4, half, pl.ds(rows - shift, 8), :]
        total = total + COEFS[shift] * pairs
    return total


class Halo:
    def __init__(self, field, landings, sems, index):
        a, b = lax.axis_index("gx"), lax.axis_index("gy")
        self.there = (b > 0, b < NY - 1, a > 0, a < NX - 1)
        self.come = (b < NY - 1, b > 0, a < NX - 1, a > 0)
        send, recv = sems
        xs, ys = pl.ds(4, 32), pl.ds(8, 32)
        faces = (
            (field.at[xs, :, pl.ds(8, 4), :], "gy", b - 1),
            (field.at[xs, :, pl.ds(36, 4), :], "gy", b + 1),
            (field.at[pl.ds(4, 4), :, ys, :], "gx", a - 1),
            (field.at[pl.ds(32, 4), :, ys, :], "gx", a + 1),
        )
        self.copies = [
            pltpu.make_async_remote_copy(
                src_ref=face, dst_ref=landing, send_sem=send.at[index, d], recv_sem=recv.at[index, d],
                device_id={axis: device}, device_id_type=MESH,
            )
            for d, ((face, axis, device), landing) in enumerate(zip(faces, landings))
        ]

    def start(self):
        for d in range(4):
            pl.when(self.there[d])(lambda: self.copies[d].start())

    def wait(self):
        for d in range(4):
            pl.when(self.come[d])(lambda: self.copies[d].wait_recv())
        for d in range(4):
            pl.when(self.there[d])(lambda: self.copies[d].wait_send())


def field_landings(field):
    xs, ys = pl.ds(4, 32), pl.ds(8, 32)
    return (
        field.at[xs, :, pl.ds(40, 4), :], field.at[xs, :, pl.ds(4, 4), :],
        field.at[pl.ds(36, 4), :, ys, :], field.at[pl.ds(0, 4), :, ys, :],
    )


def side_landings(xside, yside):
    return yside.at[1, :, :, pl.ds(8, 4), :], yside.at[0, :, :, pl.ds(4, 4), :], xside.at[1], xside.at[0]


def clear_field_edges(field):
    a, b = lax.axis_index("gx"), lax.axis_index("gy")
    for edge, low in ((a == 0, 0), (a == NX - 1, 36)):
        @pl.when(edge)
        def _():
            field[pl.ds(low, 4)] = jnp.zeros((4,) + FIELD[1:], jnp.float32)

    for edge, low in ((b == 0, 0), (b == NY - 1, 40)):
        @pl.when(edge)
        def _():
            field[:, :, pl.ds(low, 8), :] = jnp.zeros((40, 2, 8, 128), jnp.float32)


def clear_halo(field):
    for low in (0, 36):
        field[pl.ds(low, 4)] = jnp.zeros((4,) + FIELD[1:], jnp.float32)
    for low in (0, 40):
        field[pl.ds(4, 32), :, pl.ds(low, 8), :] = jnp.zeros((32, 2, 8, 128), jnp.float32)


def clear_sides(xside, yside):
    a, b = lax.axis_index("gx"), lax.axis_index("gy")
    rows = jnp.zeros((32, 2, 8, 128), jnp.float32)
    yside[0, :, :, pl.ds(8, 8), :] = rows
    yside[1, :, :, pl.ds(0, 8), :] = rows
    for edge, side, low in ((b == 0, 0, 0), (b == NY - 1, 1, 8)):
        @pl.when(edge)
        def _():
            yside[side, :, :, pl.ds(low, 8), :] = rows

    for edge, side in ((a == 0, 0), (a == NX - 1, 1)):
        @pl.when(edge)
        def _():
            xside[side] = jnp.zeros((4, 2, 32, 128), jnp.float32)


def y_face_terms(yside, x, half, tile):
    total = None
    for shift in range(1, 5):
        low = 8 - shift if tile == 0 else shift
        term = COEFS[shift] * yside[0 if tile == 0 else 1, x, half, pl.ds(low, 8), :]
        total = term if total is None else total + term
    return total


def x_face_terms(xside, side, layer, half, tile):
    total = None
    for shift in range(layer + 1, 5):
        there = 4 + layer - shift if side == 0 else shift - layer - 1
        term = COEFS[shift] * xside[side, there, half, pl.ds(tile * 8, 8), :]
        total = term if total is None else total + term
    return total


def deliver_kernel(
    traces, offsets_hbm, live_hbm, pressure_hbm, previous_hbm, courant_hbm,
    values_out, hom, pressure, courant,
    offsets, live, slots, previous, mid_values0, mid_values1, field, zterm, dz,
    load_sem, local_sem, send1, recv1, send2, recv2, send3, recv3, send4, recv4, hsend, hrecv,
):
    a, b = lax.axis_index("gx"), lax.axis_index("gy")
    loads = [
        pltpu.make_async_copy(src, dst, load_sem.at[i])
        for i, (src, dst) in enumerate((
            (offsets_hbm, offsets), (live_hbm, live), (pressure_hbm, pressure),
            (previous_hbm, previous), (courant_hbm, courant), (traces, slots.at[:, :, :, pl.ds(0, 4)]),
        ))
    ]
    for copy in loads:
        copy.start()
    sem = pltpu.get_barrier_semaphore()
    peers = [("gy", lax.rem(b + o, NY)) for o in range(1, NY)]
    peers += [("gx", lax.rem(a + o, NX)) for o in range(1, NX)]
    for axis, device in peers:
        pl.semaphore_signal(sem, inc=1, device_id={axis: device}, device_id_type=MESH)

    loads[0].wait()
    loads[1].wait()
    lane = lax.broadcasted_iota(jnp.int32, (128, 128), 1)
    counts = jnp.broadcast_to(live[...].astype(jnp.float32), (128, 128)).T.astype(jnp.int32)
    cells = offsets[...]
    margin = 8 - 4 * lax.rem(b, 2)
    code = (((cells >> 7) * 4 + margin) << 8) | jnp.where(lane < counts, cells & 127, 255)
    slots[:, :, :, 4] = code.astype(jnp.float32).reshape(8, 2, NY, 1, 128)
    loads[5].wait()
    clear_field_edges(field)
    pl.semaphore_wait(sem, len(peers))

    core, pair = lax.rem(a, 2), a // 2
    both = ((slots, mid_values0, mid_values1, values_out),)

    def remote(src, dst, send, recv, device):
        return pltpu.make_async_remote_copy(
            src_ref=src, dst_ref=dst, send_sem=send, recv_sem=recv, device_id=device, device_id_type=MESH
        )

    gy_first, gx_first, gx_second, gy_second = [], [], [], []
    own_first, own_second, own_gx_first, own_gx_second = [], [], [], []
    for kind, (given, mid0, mid1, out) in enumerate(both):
        own_first.append(pltpu.make_async_copy(given.at[:, 0, b], mid0.at[b], local_sem.at[0, kind]))
        own_gx_first.append(pltpu.make_async_copy(given.at[pair, 1], mid1.at[a], local_sem.at[1, kind]))
        own_gx_second.append(pltpu.make_async_copy(mid0.at[:, pair], out.at[a], local_sem.at[2, kind]))
        own_second.append(pltpu.make_async_copy(mid1.at[:, b], out.at[:, b], local_sem.at[3, kind]))
    for o in range(1, NY):
        to = lax.rem(b + o, NY)
        for kind, (given, mid0, mid1, out) in enumerate(both):
            gy_first.append(remote(
                given.at[:, 0, to], mid0.at[b], send1.at[o - 1, kind], recv1.at[o - 1, kind], {"gy": to}
            ))
            gy_second.append(remote(
                mid1.at[:, to], out.at[:, b], send4.at[o - 1, kind], recv4.at[o - 1, kind], {"gy": to}
            ))
    for o in range(8):
        to = lax.rem(pair + o, 8)
        for kind, (given, mid0, mid1, out) in enumerate(both):
            gx_first.append(remote(
                given.at[to, 1], mid1.at[a], send2.at[o, kind], recv2.at[o, core, kind], {"gx": 2 * to + 1}
            ))
            gx_second.append(remote(
                mid0.at[:, to], out.at[a], send3.at[o, kind], recv3.at[o, core, kind], {"gx": 2 * to}
            ))

    def gx_arrived(recv, landing):
        for o in range(8):
            for sender in range(2):
                def wait():
                    remote(landing, landing, send2.at[o, 0], recv.at[o, sender, 0], {"gx": a}).wait_recv()

                if o > 0:
                    wait()
                else:
                    pl.when(core != sender)(wait)

    for n in range(8):
        if n < 7:
            gy_first[n].start()
        if n >= 1:
            gx_first[n].start()
    for copy in own_first:
        copy.start()

    @pl.when(core == 0)
    def _():
        gx_first[0].start()

    @pl.when(core == 1)
    def _():
        own_gx_first[0].start()

    loads[2].wait()

    def load(x, _):
        for half in range(2):
            field[x + 4, half, pl.ds(8, 32), :] = pressure[x, :, half * 128 : half * 128 + 128]
        return 0

    lax.fori_loop(0, 32, load, 0)
    halo = Halo(field, field_landings(field), (hsend, hrecv), 0)
    halo.start()

    dz[...] = z_matrix()
    z_terms(field, dz, zterm)

    for copy in own_first:
        copy.wait()
    for copy in gy_first:
        copy.wait_recv()
    for copy in gx_second[1:]:
        copy.start()

    @pl.when(core == 0)
    def _():
        own_gx_second[0].start()

    @pl.when(core == 1)
    def _():
        gx_second[0].start()
        own_gx_first[0].wait()
        gx_arrived(recv2, mid_values1.at[0])
        for copy in gy_second:
            copy.start()
        for copy in own_second:
            copy.start()

    halo.wait()
    loads[3].wait()
    loads[4].wait()

    def step(x, _):
        for half in range(2):
            lanes = pl.ds(half * 128, 128)
            for tile in range(4):
                rows = pl.ds(tile * 8, 8)
                now = field[x + 4, half, pl.ds(8 + tile * 8, 8), :]
                out = 2.0 * now - previous[x, rows, lanes]
                hom[x, half, rows, :] = out + courant[x, rows, lanes] * laplacian(field, zterm, x, half, tile)
        return 0

    lax.fori_loop(0, 32, step, 0)

    for copy in gy_first:
        copy.wait_send()
    for copy in gx_first[1:]:
        copy.wait_send()
    for copy in gx_second[1:]:
        copy.wait_send()

    @pl.when(core == 0)
    def _():
        gx_first[0].wait_send()
        own_gx_second[0].wait()
        gx_arrived(recv3, values_out.at[0])

    @pl.when(core == 1)
    def _():
        gx_second[0].wait_send()
        for copy in own_second:
            copy.wait()
        for copy in gy_second:
            copy.wait()


def clear_sums(sums):
    zero = jnp.zeros((64, 128), jnp.float32)

    def clear(i, _):
        for total in sums:
            total[pl.ds(pl.multiple_of(i * 64, 64), 64), :] = zero
        return 0

    lax.fori_loop(0, 128, clear, 0)
    for total in sums:
        total[pl.ds(8192, 16), :] = jnp.zeros((16, 128), jnp.float32)


def scatter_kernel(values, *rest):
    sums = rest[:K]
    rows_all, lanes_all, rows0, rows1, lanes0, lanes1, sems = rest[K:]
    rows_all[...] = values[pl.ds(4, 128, stride=5), :].astype(jnp.int32) >> 8
    word = jnp.zeros((32, 128), jnp.int32)
    for q in range(4):
        word = word | ((values[pl.ds(5 * q + 4, 32, stride=20), :].astype(jnp.int32) & 255) << (8 * q))
    lanes_all[...] = word
    blocks = ((rows0, lanes0), (rows1, lanes1))

    def fetch(group, n):
        rows, lanes = blocks[n]
        return (
            pltpu.make_async_copy(rows_all.at[pl.ds(4 * group, 4)], rows, sems.at[n, 0]),
            pltpu.make_async_copy(lanes_all.at[pl.ds(group, 1)], lanes, sems.at[n, 1]),
        )

    for n in range(2):
        for copy in fetch(n, n):
            copy.start()
    clear_sums(sums)
    sub = lax.broadcasted_iota(jnp.int32, (8, 128), 0)
    lane = lax.broadcasted_iota(jnp.int32, (8, 128), 1)
    place = (jnp.where(sub < 4, lane, 128), jnp.where(sub < 4, 128, lane))
    place = [place[q % 2] << (8 * q) for q in range(4)]
    bits = (255, 255 << 8, 255 << 16, -(1 << 24))

    def body(i, _):
        for n in range(2):
            group = 2 * i + n
            for copy in fetch(group, n):
                copy.wait()
            rows, lanes = blocks[n]
            pairs = [
                jnp.concatenate([values[pl.ds(20 * group + 10 * p + 5 * n, 4), :] for n in range(2)], axis=0)
                for p in range(2)
            ]
            for j in range(128):
                wide = [jnp.broadcast_to(pair[:, j : j + 1], (8, 128)) for pair in pairs]
                cells = jnp.full((8, 128), lanes[0, j], jnp.int32)
                for q in range(4):
                    window = pl.ds(rows[q, j], 8)
                    total = sums[(4 * j + q) % K]
                    more = jnp.where((cells & bits[q]) == place[q], wide[q // 2], 0.0)
                    total[window, :] = total[window, :] + more

            @pl.when(i < 15)
            def _():
                for copy in fetch(group + 2, n):
                    copy.start()
        return 0

    lax.fori_loop(0, 16, body, 0)


def steps_kernel(
    *refs,
):
    sums, refs = refs[:K], refs[K:]
    (hom, pressure, courant, field_a, field_b, first, out, xside_a, yside_a, later,
     zterm, dz, xside_b, yside_b, hsend, hrecv) = refs
    a, b = lax.axis_index("gx"), lax.axis_index("gy")
    sem = pltpu.get_barrier_semaphore()
    near = (("gy", b - 1, b > 0), ("gy", b + 1, b < NY - 1), ("gx", a - 1, a > 0), ("gx", a + 1, a < NX - 1))
    for axis, device, there in near:
        @pl.when(there)
        def _():
            pl.semaphore_signal(sem, inc=1, device_id={axis: device}, device_id_type=MESH)

    def finish(i, _):
        rows = pl.ds(pl.multiple_of(i * 64 + 8, 8), 64)
        total = sums[0][rows, :]
        for other in sums[1:]:
            total = total + other[rows, :]
        turned = jnp.swapaxes(total.reshape(8, 8, 128), 0, 1)
        x, y = i // 4, i % 4 * 8
        for half in range(2):
            ys = pl.ds(pl.multiple_of(y, 8), 8)
            new = hom[x, half, ys, :] + turned[half * 4]
            first[x, half, ys, :] = new
            field_a[x + 4, half, pl.ds(pl.multiple_of(y + 8, 8), 8), :] = new
            for t in range(1, STEPS):
                later[t - 1, x, half, ys, :] = turned[half * 4 + t]
        return 0

    lax.fori_loop(0, 128, finish, 0)
    pl.semaphore_wait(sem, sum(there.astype(jnp.int32) for _, _, there in near))

    fields, sides = (field_a, field_b), ((xside_a, yside_a), (xside_b, yside_b))
    halo = Halo(field_a, side_landings(xside_a, yside_a), (hsend, hrecv), 0)
    halo.start()
    for field in fields:
        clear_halo(field)
    for side in sides:
        clear_sides(*side)
    dz[...] = z_matrix()

    for t in range(1, STEPS):
        now, nxt = fields[(t - 1) % 2], fields[t % 2]
        xside, yside = sides[(t - 1) % 2]
        last = t == STEPS - 1
        z_terms(now, dz, zterm)

        def update(x, _):
            for half in range(2):
                lanes = pl.ds(half * 128, 128)
                for tile in range(4):
                    rows, inner = pl.ds(tile * 8, 8), pl.ds(8 + tile * 8, 8)
                    centre = now[x + 4, half, inner, :]
                    before = pressure[x, rows, lanes] if t == 1 else nxt[x + 4, half, inner, :]
                    new = 2.0 * centre - before
                    new = new + courant[x, rows, lanes] * laplacian(now, zterm, x, half, tile)
                    new = new + later[t - 1, x, half, rows, :]
                    if last:
                        out[x, rows, lanes] = new
                    else:
                        nxt[x + 4, half, inner, :] = new
            return 0

        lax.fori_loop(0, 32, update, 0)
        halo.wait()
        if last:
            break

        def add(x, half, tile, terms):
            lanes, rows, inner = pl.ds(half * 128, 128), pl.ds(tile * 8, 8), pl.ds(8 + tile * 8, 8)
            more = courant[x, rows, lanes] * terms
            nxt[x + 4, half, inner, :] = nxt[x + 4, half, inner, :] + more

        def y_faces(x, _):
            for half in range(2):
                for tile in (0, 3):
                    add(x, half, tile, y_face_terms(yside, x, half, tile))
            return 0

        def x_faces(tile, _):
            for half in range(2):
                for side in range(2):
                    for layer in range(4):
                        x = layer if side == 0 else 31 - layer
                        add(x, half, tile, x_face_terms(xside, side, layer, half, tile))
            return 0

        lax.fori_loop(0, 32, y_faces, 0)
        lax.fori_loop(0, 4, x_faces, 0)
        halo = Halo(nxt, side_landings(*sides[t % 2]), (hsend, hrecv), t)
        halo.start()


def last_kernel(
    now, before, first, out, xside, yside, courant, snapshots, pressure_hbm, previous_hbm, image_hbm,
    pressure, image, out_sem,
):
    stores = [
        pltpu.make_async_copy(
            now.at[pl.ds(4, 32), half, pl.ds(8, 32), :],
            previous_hbm.at[:, :, pl.ds(half * 128, 128)], out_sem.at[half],
        )
        for half in range(2)
    ]
    for copy in stores:
        copy.start()

    def one(x, side, layer):
        for half in range(2):
            for tile in range(4):
                lanes, rows = pl.ds(half * 128, 128), pl.ds(tile * 8, 8)
                inner = pl.ds(8 + tile * 8, 8)
                new = out[x, rows, lanes]
                terms = y_face_terms(yside, x, half, tile) if tile in (0, 3) else None
                if layer is not None:
                    more = x_face_terms(xside, side, layer, half, tile)
                    terms = more if terms is None else terms + more
                if terms is not None:
                    new = new + courant[x, rows, lanes] * terms
                pressure[x, rows, lanes] = new
                seen = snapshots[0, x, rows, lanes] * first[x, half, rows, :]
                seen = seen + snapshots[1, x, rows, lanes] * before[x + 4, half, inner, :]
                seen = seen + snapshots[2, x, rows, lanes] * now[x + 4, half, inner, :]
                image[x, rows, lanes] = seen + snapshots[3, x, rows, lanes] * new

    def body(x, _):
        one(x, None, None)
        return 0

    for part in range(4):
        if part == 0:
            for layer in range(4):
                one(layer, 0, layer)
        lax.fori_loop(max(4, part * 8), min(28, part * 8 + 8), body, 0)
        if part == 3:
            for layer in range(4):
                one(31 - layer, 1, layer)
        xs = pl.ds(part * 8, 8)
        stores += [
            pltpu.make_async_copy(pressure.at[xs], pressure_hbm.at[xs], out_sem.at[2 + 2 * part]),
            pltpu.make_async_copy(image.at[xs], image_hbm.at[xs], out_sem.at[3 + 2 * part]),
        ]
        stores[-2].start()
        stores[-1].start()
    for copy in stores:
        copy.wait()


def local(pressure, previous, courant, snapshots, traces, cell_offsets, live_counts):
    f32 = jnp.float32
    vmem, anywhere = pl.BlockSpec(memory_space=pltpu.VMEM), pl.BlockSpec(memory_space=pl.ANY)
    hbm = pl.BlockSpec(memory_space=pltpu.HBM)
    dma, xside, yside = pltpu.SemaphoreType.DMA, (2, 4, 2, 32, 128), (2, 32, 2, 16, 128)
    block, wide = jax.ShapeDtypeStruct((32, 32, 256), f32), jax.ShapeDtypeStruct(FIELD, f32)
    values, hom, pressure, courant = pl.pallas_call(
        deliver_kernel,
        out_shape=(
            jax.ShapeDtypeStruct((NX, NY, 5, 1, 128), f32),
            jax.ShapeDtypeStruct(BLOCK, f32),
            block,
            block,
        ),
        in_specs=[hbm] * 6,
        out_specs=(anywhere, vmem, vmem, vmem),
        scratch_shapes=[
            pltpu.VMEM((128, 128), jnp.int32),
            pltpu.VMEM((1, 128), jnp.int32),
            pltpu.VMEM((8, 2, NY, 5, 1, 128), f32),
            pltpu.VMEM((32, 32, 256), f32),
            pltpu.VMEM((NY, 8, 5, 1, 128), f32),
            pltpu.VMEM((NX, NY, 5, 1, 128), f32),
            pltpu.VMEM(FIELD, f32),
            pltpu.VMEM(BLOCK, f32),
            pltpu.VMEM((256, 256), f32),
            dma((6,)),
            dma((4, 1)),
            dma((NY - 1, 1)),
            dma((NY - 1, 1)),
            dma((8, 1)),
            dma((8, 2, 1)),
            dma((8, 1)),
            dma((8, 2, 1)),
            dma((NY - 1, 1)),
            dma((NY - 1, 1)),
            dma((1, 4)),
            dma((1, 4)),
        ],
        compiler_params=pltpu.CompilerParams(
            collective_id=0, has_side_effects=True, vmem_limit_bytes=51300 * 1024
        ),
        name="deliver",
    )(
        traces.reshape(8, 2, NY, 4, 1, 128), cell_offsets.reshape(128, 128), live_counts,
        pressure, previous, courant,
    )
    sums = pl.pallas_call(
        scatter_kernel,
        out_shape=(jax.ShapeDtypeStruct((ROWS, 128), f32),) * K,
        in_specs=[vmem],
        out_specs=(vmem,) * K,
        scratch_shapes=[
            pltpu.VMEM((128, 128), jnp.int32),
            pltpu.VMEM((32, 128), jnp.int32),
            pltpu.SMEM((4, 128), jnp.int32),
            pltpu.SMEM((4, 128), jnp.int32),
            pltpu.SMEM((1, 128), jnp.int32),
            pltpu.SMEM((1, 128), jnp.int32),
            dma((2, 2)),
        ],
        compiler_params=pltpu.CompilerParams(vmem_limit_bytes=8000 * 1024),
        name="scatter",
    )(values.reshape(640, 128))
    now, before, first, out, xfaces, yfaces = pl.pallas_call(
        steps_kernel,
        out_shape=(
            wide,
            wide,
            jax.ShapeDtypeStruct(BLOCK, f32),
            block,
            jax.ShapeDtypeStruct(xside, f32),
            jax.ShapeDtypeStruct(yside, f32),
        ),
        in_specs=[vmem] * (K + 3),
        out_specs=(vmem,) * 6,
        scratch_shapes=[
            pltpu.VMEM((3,) + BLOCK, f32),
            pltpu.VMEM(BLOCK, f32),
            pltpu.VMEM((256, 256), f32),
            pltpu.VMEM(xside, f32),
            pltpu.VMEM(yside, f32),
            dma((3, 4)),
            dma((3, 4)),
        ],
        compiler_params=pltpu.CompilerParams(
            collective_id=1, has_side_effects=True, vmem_limit_bytes=10000 * 1024
        ),
        name="steps",
    )(*sums, hom, pressure, courant)
    return pl.pallas_call(
        last_kernel,
        out_shape=(block, block, block),
        in_specs=[vmem] * 8,
        out_specs=(hbm,) * 3,
        scratch_shapes=[pltpu.VMEM((32, 32, 256), f32)] * 2 + [dma((10,))],
        compiler_params=pltpu.CompilerParams(vmem_limit_bytes=6000 * 1024),
        name="last",
    )(now, before, first, out, xfaces, yfaces, courant, snapshots)


def solution(mesh):
    field = P("gx", "gy", None)
    return jax.shard_map(
        local,
        mesh=mesh,
        in_specs=(
            field,
            field,
            field,
            P(None, "gx", "gy", None),
            P(("gx", "gy"), None, None, None),
            P(("gx", "gy"), None, None),
            P(("gx", "gy"), None),
        ),
        out_specs=(field, field, field),
        check_vma=False,
    )
```

```python
import functools

import jax
import jax.numpy as jnp
from jax import lax
from jax.experimental import pallas as pl
from jax.experimental.pallas import tpu as pltpu
from jax.sharding import PartitionSpec as P

STEPS = 4
COEFS = (-205.0 / 72.0, 8.0 / 5.0, -1.0 / 5.0, 8.0 / 315.0, -1.0 / 560.0)
NX, NY = 16, 8
K = 6
ROWS = 8192 + 16
MESH = pl.DeviceIdType.MESH
FIELD = (40, 2, 48, 128)
BLOCK = (32, 2, 32, 128)


def barrier(peers):
    sem = pltpu.get_barrier_semaphore()
    for axis, device in peers:
        pl.semaphore_signal(sem, inc=1, device_id={axis: device}, device_id_type=MESH)
    pl.semaphore_wait(sem, len(peers))


def z_matrix():
    row = lax.broadcasted_iota(jnp.int32, (256, 256), 0)
    col = lax.broadcasted_iota(jnp.int32, (256, 256), 1)
    apart = jnp.abs(row - col)
    matrix = jnp.where(apart == 0, 3.0 * COEFS[0], 0.0)
    for shift in range(1, 5):
        matrix = jnp.where(apart == shift, COEFS[shift], matrix)
    return matrix.astype(jnp.float32)


def z_terms(field, dz, zterm):
    def body(i, _):
        xs = pl.ds(4 + i * 8, 8)
        left = field[xs, 0, pl.ds(8, 32), :].reshape(256, 128)
        right = field[xs, 1, pl.ds(8, 32), :].reshape(256, 128)
        both = jnp.concatenate([left, right], axis=1)
        out = jnp.dot(both, dz[...], precision=lax.Precision.HIGHEST, preferred_element_type=jnp.float32)
        zterm[pl.ds(i * 8, 8), 0] = out[:, :128].reshape(8, 32, 128)
        zterm[pl.ds(i * 8, 8), 1] = out[:, 128:].reshape(8, 32, 128)
        return 0

    lax.fori_loop(0, 4, body, 0)


def laplacian(field, zterm, x, half, tile):
    rows = 8 + tile * 8
    total = zterm[x, half, pl.ds(tile * 8, 8), :]
    for shift in range(1, 5):
        pairs = field[x + 4 + shift, half, pl.ds(rows, 8), :] + field[x + 4 - shift, half, pl.ds(rows, 8), :]
        pairs = pairs + field[x + 4, half, pl.ds(rows + shift, 8), :]
        pairs = pairs + field[x + 4, half, pl.ds(rows - shift, 8), :]
        total = total + COEFS[shift] * pairs
    return total


class Halo:
    def __init__(self, field, landings, sems, index):
        a, b = lax.axis_index("gx"), lax.axis_index("gy")
        self.there = (b > 0, b < NY - 1, a > 0, a < NX - 1)
        self.come = (b < NY - 1, b > 0, a < NX - 1, a > 0)
        send, recv = sems
        xs, ys = pl.ds(4, 32), pl.ds(8, 32)
        faces = (
            (field.at[xs, :, pl.ds(8, 4), :], "gy", b - 1),
            (field.at[xs, :, pl.ds(36, 4), :], "gy", b + 1),
            (field.at[pl.ds(4, 4), :, ys, :], "gx", a - 1),
            (field.at[pl.ds(32, 4), :, ys, :], "gx", a + 1),
        )
        self.copies = [
            pltpu.make_async_remote_copy(
                src_ref=face, dst_ref=landing, send_sem=send.at[index, d], recv_sem=recv.at[index, d],
                device_id={axis: device}, device_id_type=MESH,
            )
            for d, ((face, axis, device), landing) in enumerate(zip(faces, landings))
        ]

    def start(self):
        for d in range(4):
            pl.when(self.there[d])(lambda: self.copies[d].start())

    def wait(self):
        for d in range(4):
            pl.when(self.come[d])(lambda: self.copies[d].wait_recv())
        for d in range(4):
            pl.when(self.there[d])(lambda: self.copies[d].wait_send())


def side_landings(xside, yside):
    return yside.at[1, :, :, pl.ds(8, 4), :], yside.at[0, :, :, pl.ds(4, 4), :], xside.at[1], xside.at[0]


def clear_halo(field):
    for low in (0, 36):
        field[pl.ds(low, 4)] = jnp.zeros((4,) + FIELD[1:], jnp.float32)
    for low in (0, 40):
        field[pl.ds(4, 32), :, pl.ds(low, 8), :] = jnp.zeros((32, 2, 8, 128), jnp.float32)


def clear_sides(xside, yside):
    a, b = lax.axis_index("gx"), lax.axis_index("gy")
    rows = jnp.zeros((32, 2, 8, 128), jnp.float32)
    yside[0, :, :, pl.ds(8, 8), :] = rows
    yside[1, :, :, pl.ds(0, 8), :] = rows
    for edge, side, low in ((b == 0, 0, 0), (b == NY - 1, 1, 8)):
        @pl.when(edge)
        def _():
            yside[side, :, :, pl.ds(low, 8), :] = rows

    for edge, side in ((a == 0, 0), (a == NX - 1, 1)):
        @pl.when(edge)
        def _():
            xside[side] = jnp.zeros((4, 2, 32, 128), jnp.float32)


def y_face_terms(yside, x, half, tile):
    total = None
    for shift in range(1, 5):
        low = 8 - shift if tile == 0 else shift
        term = COEFS[shift] * yside[0 if tile == 0 else 1, x, half, pl.ds(low, 8), :]
        total = term if total is None else total + term
    return total


def x_face_terms(xside, side, layer, half, tile):
    total = None
    for shift in range(layer + 1, 5):
        there = 4 + layer - shift if side == 0 else shift - layer - 1
        term = COEFS[shift] * xside[side, there, half, pl.ds(tile * 8, 8), :]
        total = term if total is None else total + term
    return total


def deliver_kernel(
    traces, offsets_hbm, live_hbm, pressure_hbm, previous_hbm, courant_hbm,
    values_out, hom, pressure, courant,
    offsets, live, slots, previous, mid_values0, mid_values1, field, zterm, dz, xside, yside,
    load_sem, local_sem, send1, recv1, send2, recv2, send3, recv3, send4, recv4, hsend, hrecv,
):
    a, b = lax.axis_index("gx"), lax.axis_index("gy")
    loads = [
        pltpu.make_async_copy(src, dst, load_sem.at[i])
        for i, (src, dst) in enumerate((
            (offsets_hbm, offsets), (live_hbm, live), (pressure_hbm, pressure),
            (previous_hbm, previous), (courant_hbm, courant), (traces, slots.at[:, :, :, pl.ds(0, 4)]),
        ))
    ]
    for copy in loads:
        copy.start()
    sem = pltpu.get_barrier_semaphore()
    peers = [("gy", lax.rem(b + o, NY)) for o in range(1, NY)]
    peers += [("gx", lax.rem(a + o, NX)) for o in range(1, NX)]
    for axis, device in peers:
        pl.semaphore_signal(sem, inc=1, device_id={axis: device}, device_id_type=MESH)

    loads[0].wait()
    loads[1].wait()
    lane = lax.broadcasted_iota(jnp.int32, (128, 128), 1)
    counts = jnp.broadcast_to(live[...].astype(jnp.float32), (128, 128)).T.astype(jnp.int32)
    cells = offsets[...]
    margin = 8 - 4 * lax.rem(b, 2)
    code = (((cells >> 7) * 4 + margin) << 8) | jnp.where(lane < counts, cells & 127, 255)
    slots[:, :, :, 4] = code.astype(jnp.float32).reshape(8, 2, NY, 1, 128)
    loads[5].wait()
    clear_halo(field)
    clear_sides(xside, yside)
    pl.semaphore_wait(sem, len(peers))

    core, pair = lax.rem(a, 2), a // 2
    both = ((slots, mid_values0, mid_values1, values_out),)

    def remote(src, dst, send, recv, device):
        return pltpu.make_async_remote_copy(
            src_ref=src, dst_ref=dst, send_sem=send, recv_sem=recv, device_id=device, device_id_type=MESH
        )

    gy_first, gx_first, gx_second, gy_second = [], [], [], []
    own_first, own_second, own_gx_first, own_gx_second = [], [], [], []
    for kind, (given, mid0, mid1, out) in enumerate(both):
        own_first.append(pltpu.make_async_copy(given.at[:, 0, b], mid0.at[b], local_sem.at[0, kind]))
        own_gx_first.append(pltpu.make_async_copy(given.at[pair, 1], mid1.at[a], local_sem.at[1, kind]))
        own_gx_second.append(pltpu.make_async_copy(mid0.at[:, pair], out.at[a], local_sem.at[2, kind]))
        own_second.append(pltpu.make_async_copy(mid1.at[:, b], out.at[:, b], local_sem.at[3, kind]))
    for o in range(1, NY):
        to = lax.rem(b + o, NY)
        for kind, (given, mid0, mid1, out) in enumerate(both):
            gy_first.append(remote(
                given.at[:, 0, to], mid0.at[b], send1.at[o - 1, kind], recv1.at[o - 1, kind], {"gy": to}
            ))
            gy_second.append(remote(
                mid1.at[:, to], out.at[:, b], send4.at[o - 1, kind], recv4.at[o - 1, kind], {"gy": to}
            ))
    for o in range(8):
        to = lax.rem(pair + o, 8)
        for kind, (given, mid0, mid1, out) in enumerate(both):
            gx_first.append(remote(
                given.at[to, 1], mid1.at[a], send2.at[o, kind], recv2.at[o, core, kind], {"gx": 2 * to + 1}
            ))
            gx_second.append(remote(
                mid0.at[:, to], out.at[a], send3.at[o, kind], recv3.at[o, core, kind], {"gx": 2 * to}
            ))

    def gx_arrived(recv, landing):
        for o in range(8):
            for sender in range(2):
                def wait():
                    remote(landing, landing, send2.at[o, 0], recv.at[o, sender, 0], {"gx": a}).wait_recv()

                if o > 0:
                    wait()
                else:
                    pl.when(core != sender)(wait)

    for n in range(8):
        if n < 7:
            gy_first[n].start()
        if n >= 1:
            gx_first[n].start()
    for copy in own_first:
        copy.start()

    @pl.when(core == 0)
    def _():
        gx_first[0].start()

    @pl.when(core == 1)
    def _():
        own_gx_first[0].start()

    loads[2].wait()

    def load(x, _):
        for half in range(2):
            field[x + 4, half, pl.ds(8, 32), :] = pressure[x, :, half * 128 : half * 128 + 128]
        return 0

    lax.fori_loop(0, 32, load, 0)
    halo = Halo(field, side_landings(xside, yside), (hsend, hrecv), 0)
    halo.start()

    dz[...] = z_matrix()
    z_terms(field, dz, zterm)

    for copy in own_first:
        copy.wait()
    for copy in gy_first:
        copy.wait_recv()
    for copy in gx_second[1:]:
        copy.start()

    @pl.when(core == 0)
    def _():
        own_gx_second[0].start()

    @pl.when(core == 1)
    def _():
        gx_second[0].start()
        own_gx_first[0].wait()
        gx_arrived(recv2, mid_values1.at[0])
        for copy in gy_second:
            copy.start()
        for copy in own_second:
            copy.start()

    loads[3].wait()
    loads[4].wait()

    def step(x, _):
        for half in range(2):
            lanes = pl.ds(half * 128, 128)
            for tile in range(4):
                rows = pl.ds(tile * 8, 8)
                now = field[x + 4, half, pl.ds(8 + tile * 8, 8), :]
                out = 2.0 * now - previous[x, rows, lanes]
                hom[x, half, rows, :] = out + courant[x, rows, lanes] * laplacian(field, zterm, x, half, tile)
        return 0

    lax.fori_loop(0, 32, step, 0)
    halo.wait()

    def add(x, half, tile, terms):
        rows = pl.ds(tile * 8, 8)
        more = courant[x, rows, pl.ds(half * 128, 128)] * terms
        hom[x, half, rows, :] = hom[x, half, rows, :] + more

    def y_faces(x, _):
        for half in range(2):
            for tile in (0, 3):
                add(x, half, tile, y_face_terms(yside, x, half, tile))
        return 0

    def x_faces(tile, _):
        for half in range(2):
            for side in range(2):
                for layer in range(4):
                    x = layer if side == 0 else 31 - layer
                    add(x, half, tile, x_face_terms(xside, side, layer, half, tile))
        return 0

    lax.fori_loop(0, 32, y_faces, 0)
    lax.fori_loop(0, 4, x_faces, 0)

    for copy in gy_first:
        copy.wait_send()
    for copy in gx_first[1:]:
        copy.wait_send()
    for copy in gx_second[1:]:
        copy.wait_send()

    @pl.when(core == 0)
    def _():
        gx_first[0].wait_send()
        own_gx_second[0].wait()
        gx_arrived(recv3, values_out.at[0])

    @pl.when(core == 1)
    def _():
        gx_second[0].wait_send()
        for copy in own_second:
            copy.wait()
        for copy in gy_second:
            copy.wait()


def clear_sums(sums):
    zero = jnp.zeros((64, 128), jnp.float32)

    def clear(i, _):
        for total in sums:
            total[pl.ds(pl.multiple_of(i * 64, 64), 64), :] = zero
        return 0

    lax.fori_loop(0, 128, clear, 0)
    for total in sums:
        total[pl.ds(8192, 16), :] = jnp.zeros((16, 128), jnp.float32)


def scatter_kernel(values, *rest):
    sums = rest[:K]
    rows_all, lanes_all, rows0, rows1, lanes0, lanes1, sems = rest[K:]
    rows_all[...] = values[pl.ds(4, 128, stride=5), :].astype(jnp.int32) >> 8
    word = jnp.zeros((32, 128), jnp.int32)
    for q in range(4):
        word = word | ((values[pl.ds(5 * q + 4, 32, stride=20), :].astype(jnp.int32) & 255) << (8 * q))
    lanes_all[...] = word
    blocks = ((rows0, lanes0), (rows1, lanes1))

    def fetch(group, n):
        rows, lanes = blocks[n]
        return (
            pltpu.make_async_copy(rows_all.at[pl.ds(4 * group, 4)], rows, sems.at[n, 0]),
            pltpu.make_async_copy(lanes_all.at[pl.ds(group, 1)], lanes, sems.at[n, 1]),
        )

    for n in range(2):
        for copy in fetch(n, n):
            copy.start()
    clear_sums(sums)
    sub = lax.broadcasted_iota(jnp.int32, (8, 128), 0)
    lane = lax.broadcasted_iota(jnp.int32, (8, 128), 1)
    place = (jnp.where(sub < 4, lane, 128), jnp.where(sub < 4, 128, lane))
    place = [place[q % 2] << (8 * q) for q in range(4)]
    bits = (255, 255 << 8, 255 << 16, -(1 << 24))

    def body(i, _):
        for n in range(2):
            group = 2 * i + n
            for copy in fetch(group, n):
                copy.wait()
            rows, lanes = blocks[n]
            pairs = [
                jnp.concatenate([values[pl.ds(20 * group + 10 * p + 5 * n, 4), :] for n in range(2)], axis=0)
                for p in range(2)
            ]
            for j in range(128):
                wide = [jnp.broadcast_to(pair[:, j : j + 1], (8, 128)) for pair in pairs]
                cells = jnp.full((8, 128), lanes[0, j], jnp.int32)
                for q in range(4):
                    window = pl.ds(rows[q, j], 8)
                    total = sums[(4 * j + q) % K]
                    more = jnp.where((cells & bits[q]) == place[q], wide[q // 2], 0.0)
                    total[window, :] = total[window, :] + more

            @pl.when(i < 15)
            def _():
                for copy in fetch(group + 2, n):
                    copy.start()
        return 0

    lax.fori_loop(0, 16, body, 0)


def steps_kernel(
    *refs,
):
    sums, refs = refs[:K], refs[K:]
    (hom, pressure, courant, field_a, field_b, first, out, xside_a, yside_a, later,
     zterm, dz, xside_b, yside_b, hsend, hrecv) = refs
    a, b = lax.axis_index("gx"), lax.axis_index("gy")
    sem = pltpu.get_barrier_semaphore()
    near = (("gy", b - 1, b > 0), ("gy", b + 1, b < NY - 1), ("gx", a - 1, a > 0), ("gx", a + 1, a < NX - 1))
    for axis, device, there in near:
        @pl.when(there)
        def _():
            pl.semaphore_signal(sem, inc=1, device_id={axis: device}, device_id_type=MESH)

    def finish(i, _):
        rows = pl.ds(pl.multiple_of(i * 64 + 8, 8), 64)
        total = sums[0][rows, :]
        for other in sums[1:]:
            total = total + other[rows, :]
        turned = jnp.swapaxes(total.reshape(8, 8, 128), 0, 1)
        x, y = i // 4, i % 4 * 8
        for half in range(2):
            ys = pl.ds(pl.multiple_of(y, 8), 8)
            new = hom[x, half, ys, :] + turned[half * 4]
            first[x, half, ys, :] = new
            field_a[x + 4, half, pl.ds(pl.multiple_of(y + 8, 8), 8), :] = new
            for t in range(1, STEPS):
                later[t - 1, x, half, ys, :] = turned[half * 4 + t]
        return 0

    lax.fori_loop(0, 128, finish, 0)
    pl.semaphore_wait(sem, sum(there.astype(jnp.int32) for _, _, there in near))

    fields, sides = (field_a, field_b), ((xside_a, yside_a), (xside_b, yside_b))
    halo = Halo(field_a, side_landings(xside_a, yside_a), (hsend, hrecv), 0)
    halo.start()
    for field in fields:
        clear_halo(field)
    for side in sides:
        clear_sides(*side)
    dz[...] = z_matrix()

    for t in range(1, STEPS):
        now, nxt = fields[(t - 1) % 2], fields[t % 2]
        xside, yside = sides[(t - 1) % 2]
        last = t == STEPS - 1
        z_terms(now, dz, zterm)

        def update(x, _):
            for half in range(2):
                lanes = pl.ds(half * 128, 128)
                for tile in range(4):
                    rows, inner = pl.ds(tile * 8, 8), pl.ds(8 + tile * 8, 8)
                    centre = now[x + 4, half, inner, :]
                    before = pressure[x, rows, lanes] if t == 1 else nxt[x + 4, half, inner, :]
                    new = 2.0 * centre - before
                    new = new + courant[x, rows, lanes] * laplacian(now, zterm, x, half, tile)
                    new = new + later[t - 1, x, half, rows, :]
                    if last:
                        out[x, rows, lanes] = new
                    else:
                        nxt[x + 4, half, inner, :] = new
            return 0

        lax.fori_loop(0, 32, update, 0)
        halo.wait()
        if last:
            break

        def add(x, half, tile, terms):
            lanes, rows, inner = pl.ds(half * 128, 128), pl.ds(tile * 8, 8), pl.ds(8 + tile * 8, 8)
            more = courant[x, rows, lanes] * terms
            nxt[x + 4, half, inner, :] = nxt[x + 4, half, inner, :] + more

        def y_faces(x, _):
            for half in range(2):
                for tile in (0, 3):
                    add(x, half, tile, y_face_terms(yside, x, half, tile))
            return 0

        def x_faces(tile, _):
            for half in range(2):
                for side in range(2):
                    for layer in range(4):
                        x = layer if side == 0 else 31 - layer
                        add(x, half, tile, x_face_terms(xside, side, layer, half, tile))
            return 0

        lax.fori_loop(0, 32, y_faces, 0)
        lax.fori_loop(0, 4, x_faces, 0)
        halo = Halo(nxt, side_landings(*sides[t % 2]), (hsend, hrecv), t)
        halo.start()


def last_kernel(
    now, before, first, out, xside, yside, courant, snapshots, pressure_hbm, previous_hbm, image_hbm,
    pressure, image, out_sem,
):
    stores = [
        pltpu.make_async_copy(
            now.at[pl.ds(4, 32), half, pl.ds(8, 32), :],
            previous_hbm.at[:, :, pl.ds(half * 128, 128)], out_sem.at[half],
        )
        for half in range(2)
    ]
    for copy in stores:
        copy.start()

    def one(x, side, layer):
        for half in range(2):
            for tile in range(4):
                lanes, rows = pl.ds(half * 128, 128), pl.ds(tile * 8, 8)
                inner = pl.ds(8 + tile * 8, 8)
                new = out[x, rows, lanes]
                terms = y_face_terms(yside, x, half, tile) if tile in (0, 3) else None
                if layer is not None:
                    more = x_face_terms(xside, side, layer, half, tile)
                    terms = more if terms is None else terms + more
                if terms is not None:
                    new = new + courant[x, rows, lanes] * terms
                pressure[x, rows, lanes] = new
                seen = snapshots[0, x, rows, lanes] * first[x, half, rows, :]
                seen = seen + snapshots[1, x, rows, lanes] * before[x + 4, half, inner, :]
                seen = seen + snapshots[2, x, rows, lanes] * now[x + 4, half, inner, :]
                image[x, rows, lanes] = seen + snapshots[3, x, rows, lanes] * new

    def body(x, _):
        one(x, None, None)
        return 0

    for part in range(4):
        if part == 0:
            for layer in range(4):
                one(layer, 0, layer)
        lax.fori_loop(max(4, part * 8), min(28, part * 8 + 8), body, 0)
        if part == 3:
            for layer in range(4):
                one(31 - layer, 1, layer)
        xs = pl.ds(part * 8, 8)
        stores += [
            pltpu.make_async_copy(pressure.at[xs], pressure_hbm.at[xs], out_sem.at[2 + 2 * part]),
            pltpu.make_async_copy(image.at[xs], image_hbm.at[xs], out_sem.at[3 + 2 * part]),
        ]
        stores[-2].start()
        stores[-1].start()
    for copy in stores:
        copy.wait()


def local(pressure, previous, courant, snapshots, traces, cell_offsets, live_counts):
    f32 = jnp.float32
    vmem, anywhere = pl.BlockSpec(memory_space=pltpu.VMEM), pl.BlockSpec(memory_space=pl.ANY)
    hbm = pl.BlockSpec(memory_space=pltpu.HBM)
    dma, xside, yside = pltpu.SemaphoreType.DMA, (2, 4, 2, 32, 128), (2, 32, 2, 16, 128)
    block, wide = jax.ShapeDtypeStruct((32, 32, 256), f32), jax.ShapeDtypeStruct(FIELD, f32)
    values, hom, pressure, courant = pl.pallas_call(
        deliver_kernel,
        out_shape=(
            jax.ShapeDtypeStruct((NX, NY, 5, 1, 128), f32),
            jax.ShapeDtypeStruct(BLOCK, f32),
            block,
            block,
        ),
        in_specs=[hbm] * 6,
        out_specs=(anywhere, vmem, vmem, vmem),
        scratch_shapes=[
            pltpu.VMEM((128, 128), jnp.int32),
            pltpu.VMEM((1, 128), jnp.int32),
            pltpu.VMEM((8, 2, NY, 5, 1, 128), f32),
            pltpu.VMEM((32, 32, 256), f32),
            pltpu.VMEM((NY, 8, 5, 1, 128), f32),
            pltpu.VMEM((NX, NY, 5, 1, 128), f32),
            pltpu.VMEM(FIELD, f32),
            pltpu.VMEM(BLOCK, f32),
            pltpu.VMEM((256, 256), f32),
            pltpu.VMEM(xside, f32),
            pltpu.VMEM(yside, f32),
            dma((6,)),
            dma((4, 1)),
            dma((NY - 1, 1)),
            dma((NY - 1, 1)),
            dma((8, 1)),
            dma((8, 2, 1)),
            dma((8, 1)),
            dma((8, 2, 1)),
            dma((NY - 1, 1)),
            dma((NY - 1, 1)),
            dma((1, 4)),
            dma((1, 4)),
        ],
        compiler_params=pltpu.CompilerParams(
            collective_id=0, has_side_effects=True, vmem_limit_bytes=51300 * 1024
        ),
        name="deliver",
    )(
        traces.reshape(8, 2, NY, 4, 1, 128), cell_offsets.reshape(128, 128), live_counts,
        pressure, previous, courant,
    )
    sums = pl.pallas_call(
        scatter_kernel,
        out_shape=(jax.ShapeDtypeStruct((ROWS, 128), f32),) * K,
        in_specs=[vmem],
        out_specs=(vmem,) * K,
        scratch_shapes=[
            pltpu.VMEM((128, 128), jnp.int32),
            pltpu.VMEM((32, 128), jnp.int32),
            pltpu.SMEM((4, 128), jnp.int32),
            pltpu.SMEM((4, 128), jnp.int32),
            pltpu.SMEM((1, 128), jnp.int32),
            pltpu.SMEM((1, 128), jnp.int32),
            dma((2, 2)),
        ],
        compiler_params=pltpu.CompilerParams(vmem_limit_bytes=8000 * 1024),
        name="scatter",
    )(values.reshape(640, 128))
    now, before, first, out, xfaces, yfaces = pl.pallas_call(
        steps_kernel,
        out_shape=(
            wide,
            wide,
            jax.ShapeDtypeStruct(BLOCK, f32),
            block,
            jax.ShapeDtypeStruct(xside, f32),
            jax.ShapeDtypeStruct(yside, f32),
        ),
        in_specs=[vmem] * (K + 3),
        out_specs=(vmem,) * 6,
        scratch_shapes=[
            pltpu.VMEM((3,) + BLOCK, f32),
            pltpu.VMEM(BLOCK, f32),
            pltpu.VMEM((256, 256), f32),
            pltpu.VMEM(xside, f32),
            pltpu.VMEM(yside, f32),
            dma((3, 4)),
            dma((3, 4)),
        ],
        compiler_params=pltpu.CompilerParams(
            collective_id=1, has_side_effects=True, vmem_limit_bytes=10000 * 1024
        ),
        name="steps",
    )(*sums, hom, pressure, courant)
    return pl.pallas_call(
        last_kernel,
        out_shape=(block, block, block),
        in_specs=[vmem] * 8,
        out_specs=(hbm,) * 3,
        scratch_shapes=[pltpu.VMEM((32, 32, 256), f32)] * 2 + [dma((10,))],
        compiler_params=pltpu.CompilerParams(vmem_limit_bytes=6000 * 1024),
        name="last",
    )(now, before, first, out, xfaces, yfaces, courant, snapshots)


def solution(mesh):
    field = P("gx", "gy", None)
    return jax.shard_map(
        local,
        mesh=mesh,
        in_specs=(
            field,
            field,
            field,
            P(None, "gx", "gy", None),
            P(("gx", "gy"), None, None, None),
            P(("gx", "gy"), None, None),
            P(("gx", "gy"), None),
        ),
        out_specs=(field, field, field),
        check_vma=False,
    )
```
